256 devices in a mesh: ctx: 32 (over z, x_hi, core), head: 8 (over x_lo, y).
Axes of the slice: x: 4 (x_hi: 2, x_lo: 2; x = x_hi * 2 + x_lo), y: 4, z: 8, core: 2. Of those that a mesh axis runs over, the one named last changes fastest.
Arguments:
- queries: bfloat16 [4096, 12288], P('ctx', 'head'), may hold values from -256 to 256
- latent_rope: bfloat16 [4096, 576], P('ctx'), may hold values from -8 to 8
- key_up: bfloat16 [512, 8192], P(None, 'head'), may hold values from -0.25 to 0.25
- value_up: bfloat16 [512, 8192], P(None, 'head'), may hold values from -0.25 to 0.25
- out_weight: bfloat16 [8192, 7168], P('head', 'ctx'), may hold values from -1 to 1
- plan: int32 [32, 2], replicated, may hold values from 0 to 63, as said below
Outputs:
- mixed: bfloat16 [4096, 7168], P('ctx', 'head')
The draws below stay inside these ranges and needn't reach their ends.
Inputs may be any that keep to these rules, and one draw needn't show every extreme that they name: `plan`: row c names the two blocks of 64 consecutive positions held by device c of ctx, in the order of its rows; the two add up to 63, and every block appears once.
All inputs are finite; a program needn't handle non-finite values.
Results may differ from the reference program's by a relative error of at most 0.018.
Values may be sent and summed in bfloat16 or wider, within the bound.
A program may use at most 128 MiB of HBM per device.

```python
import jax
import jax.numpy as jnp
from jax import lax

D = 7168
HEADS = 64
NOPE = 128
ROPE = 64
VDIM = 128
LATENT = 512
TOK_DEV = 128
TOKENS = 4096
N_HEAD = 8


def plan_of(key):
    devices = TOKENS // TOK_DEV
    pick_key, flip_key = jax.random.split(jax.random.fold_in(key, 11))
    lower_ids = jax.random.permutation(pick_key, devices).astype(jnp.int32)
    upper_ids = (2 * devices - 1 - lower_ids).astype(jnp.int32)
    swapped = jax.random.randint(flip_key, (devices,), 0, 2).astype(jnp.int32)
    first_ids = jnp.where(swapped == 1, upper_ids, lower_ids)
    second_ids = jnp.where(swapped == 1, lower_ids, upper_ids)
    return jnp.stack([first_ids, second_ids], axis=1).astype(jnp.int32)


def draw_plan(key, part):
    return plan_of(key)


def draw_latent_rope(key, part):
    key = jax.random.fold_in(key, 5)
    values = jax.random.truncated_normal(key, -6.0, 6.0, (TOKENS, LATENT + ROPE), jnp.float32)
    return values.astype(jnp.bfloat16)


def draw_queries(key, part):
    key = jax.random.fold_in(key, 7)
    values = 1.5 * jax.random.truncated_normal(key, -6.0, 6.0, (TOKENS, HEADS, NOPE + ROPE), jnp.float32)
    return values.reshape(TOKENS, HEADS * (NOPE + ROPE)).astype(jnp.bfloat16)


def spiked(entries, stream_key, source, target, blocks, factor):
    def block_of(axis_at):
        return (jnp.arange(entries.shape[axis_at]) // (entries.shape[axis_at] // blocks)).reshape((-1,) + (1,) * (entries.ndim - 1 - axis_at))

    one_side = jax.random.permutation(stream_key, blocks)[block_of(target)]
    second = (block_of(target) + blocks // 2) % blocks
    return jnp.where((block_of(source) == one_side) | (block_of(source) == second), factor * entries, entries)


def steps_of(key, shape, pieces, smallest, high):
    level, own = 1.0, jax.random.fold_in(key, 6)
    for axis_at, parts in pieces:
        heights = jnp.exp(jax.random.uniform(jax.random.fold_in(own, axis_at), (parts,), jnp.float32, smallest / len(pieces), high / len(pieces)))
        level = level * jnp.repeat(heights, shape[axis_at] // parts).reshape([-1 if axis == axis_at else 1 for axis in range(len(shape))])
    return level


def noise(own_key, extent, scale, most, shards=(), kind=jnp.bfloat16):
    drawn = scale * jax.random.normal(own_key, extent, jnp.float32)
    if shards:
        drawn = drawn * steps_of(own_key, extent, shards, -0.22, 0.18)
    return jnp.clip(drawn, -most, most).astype(kind)


def bell_draw_with(own_key, dims, scale, limit, shards, heavy, kind=jnp.bfloat16):
    array = scale * jax.random.normal(own_key, dims, jnp.float32)
    if shards:
        array = array * steps_of(own_key, dims, shards, -0.22, 0.18)
    return jnp.clip(spiked(array, jax.random.fold_in(own_key, 3), *heavy), -limit, limit).astype(kind)


def setup_inputs(seed: int = 0) -> dict:
    seeds = jax.random.split(jax.random.key(seed), 7)
    queries = draw_queries(jax.random.fold_in(seeds[6], 71), 0)
    latent_rope = draw_latent_rope(jax.random.fold_in(seeds[6], 71), 0)
    key_up = noise(seeds[2], (LATENT, HEADS * NOPE), LATENT ** -0.5, 0.25, ((1, 8),))
    value_up = noise(seeds[3], (LATENT, HEADS * VDIM), LATENT ** -0.5, 0.25, ((1, 8),))
    out_weight = bell_draw_with(seeds[4], (HEADS * VDIM, D), (HEADS * VDIM // 64) ** -0.5, 1.0, ((0, 8), (1, 32)), (0, 1, 32, 2.75))
    plan = draw_plan(jax.random.fold_in(seeds[6], 71), 0)
    return {"queries": queries, "latent_rope": latent_rope, "key_up": key_up, "value_up": value_up, "out_weight": out_weight, "plan": plan}


def reference(queries, latent_rope, key_up, value_up, out_weight, plan):
    half_rows = TOK_DEV // 2
    row_ids = jnp.arange(TOKENS, dtype=jnp.int32)
    slot_index = (row_ids // TOK_DEV) * 2 + (row_ids % TOK_DEV) // half_rows
    block_ids = plan.reshape(-1)[slot_index]
    positions = (block_ids * half_rows + row_ids % half_rows).astype(jnp.int32)
    latent_only = latent_rope[:, :LATENT]
    rope_rows = latent_rope[:, LATENT:]
    key_rows = jnp.dot(latent_only, key_up, preferred_element_type=jnp.float32).astype(jnp.bfloat16)
    value_rows = jnp.dot(latent_only, value_up, preferred_element_type=jnp.float32).astype(jnp.bfloat16)
    allowed = positions[:, None] >= positions[None, :]
    score_scale = (NOPE + ROPE) ** -0.5

    def one_head(head_index):
        query_head = lax.dynamic_slice_in_dim(queries, head_index * (NOPE + ROPE), NOPE + ROPE, 1)
        key_head = lax.dynamic_slice_in_dim(key_rows, head_index * NOPE, NOPE, 1)
        value_head = lax.dynamic_slice_in_dim(value_rows, head_index * VDIM, VDIM, 1)
        scores = jnp.dot(query_head[:, :NOPE], key_head.T, preferred_element_type=jnp.float32)
        scores = scores + jnp.dot(query_head[:, NOPE:], rope_rows.T, preferred_element_type=jnp.float32)
        scores = scores * score_scale
        scores = jnp.where(allowed, scores, -1e30)
        row_max = jnp.max(scores, axis=1, keepdims=True)
        weights = jnp.where(allowed, jnp.exp(scores - row_max), 0.0)
        row_sum = jnp.sum(weights, axis=1, keepdims=True)
        weights_rounded = weights.astype(jnp.bfloat16)
        summed = jnp.dot(weights_rounded, value_head, preferred_element_type=jnp.float32)
        return (summed / row_sum).astype(jnp.bfloat16)

    per_head = lax.map(one_head, jnp.arange(HEADS, dtype=jnp.int32))
    attended = jnp.transpose(per_head, (1, 0, 2)).reshape(TOKENS, HEADS * VDIM)
    group_width = HEADS * VDIM // N_HEAD
    mixed = jnp.zeros((TOKENS, D), jnp.float32)
    for group_index in range(N_HEAD):
        lower = group_index * group_width
        head_partial = jnp.dot(attended[:, lower:lower + group_width], out_weight[lower:lower + group_width, :], preferred_element_type=jnp.float32).astype(jnp.bfloat16)
        mixed = mixed + head_partial.astype(jnp.float32)
    return mixed.astype(jnp.bfloat16)
```

```python
import functools

import jax
import jax.numpy as jnp
from jax import lax
from jax.experimental import pallas as pl
from jax.experimental.pallas import tpu as pltpu
from jax.sharding import PartitionSpec as P

MESH = pl.DeviceIdType.MESH
NOPE = 128
ROPE = 64
VDIM = 128
LATENT = 512
HEAD_LOCAL = 8
GROUP = 4
BLOCK = 64
TASKS = 17
WIDE = 640
NEG = -1e30
SCALE2 = 1.4426950408889634 * (NOPE + ROPE) ** -0.5


def nt(a, b):
    return lax.dot_general(a, b, (((1,), (1,)), ((), ())), preferred_element_type=jnp.float32)


def kernel(
    plan_ref, inv_ref, q_ref, lr_ref, ku_ref, vu_ref, w_ref, out_ref,
    lat, qs, sbuf, mrun, mfin, lrun, acc, wt, wbuf, att, csend, crecv, fsend, frecv,
    zs, zr, xs, xr, ys, yr, ks, kr, w0, ws, wr, as_, ar, bs, br, cs, cr, fs, fr,
):
    ctx = lax.axis_index("ctx")
    head = lax.axis_index("head")
    core = lax.rem(ctx, 2)
    xh = lax.rem(ctx // 2, 2)
    z = ctx // 4
    xl = head // 4
    y = lax.rem(head, 4)
    x = xh * 2 + xl

    def dev(z_, x_, y_, c_):
        return ((z_ * 2 + x_ // 2) * 2 + c_, lax.rem(x_, 2) * 4 + y_)

    def zdev(d):
        return dev(lax.rem(z + d, 8), x, y, core)

    def xdev(o):
        return dev(z, lax.rem(x + o, 4), y, core)

    def ydev(o):
        return dev(z, x, lax.rem(y + o, 4), core)

    other = dev(z, x, y, 1 - core)

    def rcopy(src, dst, ssem, rsem, target):
        return pltpu.make_async_remote_copy(
            src_ref=src, dst_ref=dst, send_sem=ssem, recv_sem=rsem,
            device_id=target, device_id_type=MESH,
        )

    barrier = pltpu.get_barrier_semaphore()
    for d in range(1, 8):
        pl.semaphore_signal(barrier, 1, device_id=zdev(d), device_id_type=MESH)
    for o in range(1, 4):
        pl.semaphore_signal(barrier, 1, device_id=ydev(o), device_id_type=MESH)
    for o in range(4):
        if o:
            pl.semaphore_signal(barrier, 1, device_id=xdev(o), device_id_type=MESH)
        pl.semaphore_signal(
            barrier, 1, device_id=dev(z, lax.rem(x + o, 4), y, 1 - core), device_id_type=MESH
        )

    par = lax.rem(y, 2)

    def piece(src_x, parity, c_):
        return (src_x // 2) * 8 + c_ * 4 + parity * 2 + lax.rem(src_x, 2)

    mine = piece(x, par, core)
    block = lr_ref[pl.ds((par * 2 + xl) * 32, 32), :]
    lat[z, mine, :, 0:LATENT] = block[:, :LATENT]
    lat[z, mine, :, LATENT:WIDE] = jnp.concatenate(
        [block[:, LATENT:], jnp.zeros((32, WIDE - LATENT - ROPE), jnp.bfloat16)], axis=1
    )
    pl.semaphore_wait(barrier, 17)

    zcopies = []
    for d in range(1, 8):
        cp = rcopy(lat.at[z, mine], lat.at[z, mine], zs.at[d - 1], zr.at[d - 1], zdev(d))
        cp.start()
        zcopies.append(cp)

    wt[...] = jnp.transpose(w_ref[...], (1, 0))
    wj = lax.rem(z, 4)
    keeper = z // 4
    at_home = jnp.logical_and(core == xl, core == keeper)

    @pl.when(at_home)
    def _():
        pltpu.make_async_copy(wt, wbuf.at[wj, xl], wr.at[wj, xl]).start()

    @pl.when(jnp.logical_not(at_home))
    def _():
        rcopy(
            wt, wbuf.at[wj, xl], w0.at[0], wr.at[wj, xl], dev(z, xh * 2 + core, y, keeper)
        ).start()

    for h in range(HEAD_LOCAL):
        lo = h * (NOPE + ROPE)
        qn = q_ref[:, lo : lo + NOPE]
        qr = q_ref[:, lo + NOPE : lo + NOPE + ROPE]
        ql = nt(qn, ku_ref[:, h * NOPE : (h + 1) * NOPE]).astype(jnp.bfloat16)
        qr = jnp.concatenate([qr, jnp.zeros((2 * BLOCK, WIDE - LATENT - ROPE), jnp.bfloat16)], axis=1)
        g, r = h // GROUP, (h % GROUP) * BLOCK
        for i in range(2):
            qs[g, i, r : r + BLOCK, 0:LATENT] = ql[i * BLOCK : (i + 1) * BLOCK]
            qs[g, i, r : r + BLOCK, LATENT:WIDE] = qr[i * BLOCK : (i + 1) * BLOCK]

    for cp in zcopies:
        cp.wait()

    pending = []

    def region(idx):
        return lat.at[pl.ds(0, 8), idx]

    def half(idx, hz):
        return lat.at[pl.ds(4 * hz, 4), idx]

    def spread(o):
        src_x = lax.rem(x + 4 - o, 4)
        idx = piece(src_x, par, core)
        for n in range(2):
            cp = rcopy(half(idx, n), half(idx, n), ys.at[o, n], yr.at[o, n], ydev(1 + 2 * n))
            cp.start()
            pending.append(cp)
        cp = rcopy(region(idx), region(idx), ks.at[o, 0], kr.at[o, 0], other)
        cp.start()
        pending.append(cp)

    def ring_send(j, part, up):
        slot = wbuf.at[j, part]
        n = 0 if up else 1
        rcopy(slot, slot, ws.at[n, j, part], wr.at[j, part], zdev(1 if up else 7)).start()

    def ring_wait(j, part):
        slot = wbuf.at[j, part]
        rcopy(slot, slot, w0.at[0], wr.at[j, part], other).wait_recv()

    def ring_step(s):
        if s == 0:
            @pl.when(core == keeper)
            def _():
                for part in range(2):
                    ring_wait(wj, part)
                for part in range(2):
                    ring_send(wj, part, True)
                    ring_send(wj, part, False)
            return
        for up in (True, False):
            zsrc = lax.rem(z + (8 - s if up else s), 8)
            j = lax.rem(zsrc, 4)

            @pl.when(core == zsrc // 4)
            def _():
                far = 0 if up else 1
                if s <= 4:
                    ring_wait(j, far)
                if s <= 3:
                    ring_wait(j, 1 - far)
                if s < 4:
                    ring_send(j, far, up)
                if s < 3:
                    ring_send(j, 1 - far, up)

    xcopies = []
    for o in (1, 3, 2):
        cp = rcopy(region(mine), region(mine), xs.at[o - 1], xr.at[o - 1], xdev(o))
        cp.start()
        xcopies.append((o, cp))
    spread(0)
    ring_step(0)
    for o, cp in xcopies:
        cp.wait()
        spread(o)
    ycopies = []
    for o in (0, 1, 3, 2):
        src_x = lax.rem(x + 4 - o, 4)
        idx = piece(src_x, 1 - par, core)
        for n in range(2):
            rcopy(half(idx, n), half(idx, n), ys.at[o, n], yr.at[o, n], other).wait_recv()
        cp = rcopy(region(idx), region(idx), ks.at[o, 1], kr.at[o, 1], other)
        cp.start()
        ycopies.append(cp)
    for cp in pending:
        cp.wait_send()
    for o in range(4):
        src_x = lax.rem(x + 4 - o, 4)
        for n, parity in ((0, par), (1, 1 - par)):
            idx = piece(src_x, parity, 1 - core)
            rcopy(region(idx), region(idx), ks.at[o, n], kr.at[o, n], other).wait_recv()
    for cp in ycopies:
        cp.wait_send()

    p0 = plan_ref[ctx, 0]
    p1 = plan_ref[ctx, 1]
    low = jnp.minimum(p0, p1)
    high = jnp.maximum(p0, p1)
    low_at = jnp.where(p0 < p1, 0, 1)
    beta = lax.div(low, 4)
    rows = GROUP * BLOCK
    row_of = lax.broadcasted_iota(jnp.int32, (rows, 256), 0) % BLOCK
    lane_of = lax.broadcasted_iota(jnp.int32, (rows, 256), 1)
    ahead = lane_of - row_of

    def chunk_of(t):
        return jnp.where(t <= beta, t, t - beta - 1)

    def keys_of(t):
        first = chunk_of(t) * 4
        got = []
        for i in range(4):
            s = inv_ref[first + i]
            got.append(lat[lax.div(s, 8), pl.ds(lax.rem(s, 8) * 2, 2)].reshape(BLOCK, WIDE))
        return jnp.concatenate(got, axis=0)

    for g in range(2):
        mrun[0] = jnp.full((rows, 128), NEG, jnp.float32)
        lrun[0] = jnp.zeros((rows, 128), jnp.float32)
        acc[0] = jnp.zeros((rows, LATENT), jnp.float32)

        def score(t, carry):
            is_low = t <= beta
            q = qs[g, jnp.where(is_low, low_at, 1 - low_at)]
            s = nt(q, keys_of(t)) * SCALE2
            room = jnp.where(is_low, low, high) * BLOCK - chunk_of(t) * 256
            s = jnp.where(ahead <= room, s, NEG)
            sbuf[t] = s
            before = jnp.where(t == beta + 1, NEG, mrun[t])
            mrun[t + 1] = jnp.maximum(before, jnp.maximum(s[:, :128], s[:, 128:]))
            return carry

        lax.fori_loop(0, TASKS, score, 0)
        mfin[0] = jnp.broadcast_to(jnp.max(mrun[beta + 1], axis=1, keepdims=True), (rows, 128))
        mfin[1] = jnp.broadcast_to(jnp.max(mrun[TASKS], axis=1, keepdims=True), (rows, 128))

        def weigh(t, carry):
            is_low = t <= beta
            keep = jnp.where(t == beta + 1, 0.0, 1.0)
            m = mfin[jnp.where(is_low, 0, 1)]
            s = sbuf[t]
            wa = jnp.exp2(s[:, :128] - m)
            wb = jnp.exp2(s[:, 128:] - m)
            lrun[t + 1] = lrun[t] * keep + (wa + wb)
            w = jnp.concatenate([wa, wb], axis=1).astype(jnp.bfloat16)
            added = jnp.dot(w, keys_of(t)[:, :LATENT], preferred_element_type=jnp.float32)
            acc[t + 1] = acc[t] * keep + added
            return carry

        lax.fori_loop(0, TASKS, weigh, 0)

        def normal(at):
            total = jnp.sum(lrun[at], axis=1, keepdims=True)
            return (acc[at] / total).astype(jnp.bfloat16)

        o_low = normal(beta + 1)
        o_high = normal(TASKS)
        first = jnp.where(low_at == 0, o_low, o_high)
        second = jnp.where(low_at == 0, o_high, o_low)
        for hh in range(GROUP):
            h = g * GROUP + hh
            r = slice(hh * BLOCK, (hh + 1) * BLOCK)
            o = jnp.concatenate([first[r], second[r]], axis=0)
            up = jnp.dot(o, vu_ref[:, h * VDIM : (h + 1) * VDIM], preferred_element_type=jnp.float32)
            att[xl, xh, core, :, h * VDIM : (h + 1) * VDIM] = up.astype(jnp.bfloat16)

        def shard(src_x, c_):
            return att.at[
                lax.rem(src_x, 2), src_x // 2, c_, :, pl.ds(g * GROUP * VDIM, GROUP * VDIM)
            ]

        for o in (1, 3, 2):
            rcopy(shard(x, core), shard(x, core), as_.at[g, o - 1], ar.at[g, o - 1], xdev(o)).start()
        rcopy(shard(x, core), shard(x, core), bs.at[g, 0], br.at[g, 0], other).start()
        ring_step(g + 1)

    for g in range(2):
        def shard(src_x, c_):
            return att.at[
                lax.rem(src_x, 2), src_x // 2, c_, :, pl.ds(g * GROUP * VDIM, GROUP * VDIM)
            ]

        for o in (1, 3, 2):
            there = shard(lax.rem(x + 4 - o, 4), core)
            cp = rcopy(there, there, as_.at[g, o - 1], ar.at[g, o - 1], other)
            cp.wait_recv()
            cp.wait_send()
            rcopy(there, there, bs.at[g, o], br.at[g, o], other).start()
    for g in range(2):
        for o in range(4):
            def shard(src_x, c_):
                return att.at[
                    lax.rem(src_x, 2), src_x // 2, c_, :, pl.ds(g * GROUP * VDIM, GROUP * VDIM)
                ]

            there = shard(lax.rem(x + 4 - o, 4), 1 - core)
            cp = rcopy(there, there, bs.at[g, o], br.at[g, o], other)
            cp.wait_recv()
            cp.wait_send()

    def project(zsrc):
        j = lax.rem(zsrc, 4)

        @pl.when(core == zsrc // 4)
        def _():
            total = nt(wbuf[j, 0], att[0].reshape(512, 1024)) + nt(
                wbuf[j, 1], att[1].reshape(512, 1024)
            )
            csend[j] = total.astype(jnp.bfloat16)
            o = lax.rem(j + 4 - y, 4)

            @pl.when(o != 0)
            def _():
                rcopy(csend.at[j], crecv.at[o], cs.at[o], cr.at[o], dev(z, x, j, core)).start()

    def two(s, carry):
        project(lax.rem(z + 8 - s, 8))
        project(lax.rem(z + s, 8))
        return carry

    project(z)
    lax.fori_loop(1, 3, two, 0)
    ring_step(3)
    lax.fori_loop(3, 4, two, 0)
    ring_step(4)
    project(lax.rem(z + 4, 8))

    for o in range(1, 4):
        cp = rcopy(csend.at[0], crecv.at[o], cs.at[o], cr.at[o], other)
        cp.wait_recv()
        cp.wait_send()
    summed = csend[y].astype(jnp.float32)
    for o in range(1, 4):
        summed = summed + crecv[o].astype(jnp.float32)
    summed = summed.astype(jnp.bfloat16)
    for n in range(4):
        fsend[n] = summed[:, n * 128 : (n + 1) * 128]
    for n in range(4):
        to_x = (n // 2) * 2 + core
        local = jnp.logical_and(to_x == x, core == n % 2)

        @pl.when(local)
        def _():
            pltpu.make_async_copy(fsend.at[n], frecv.at[x], fr.at[x]).start()

        @pl.when(jnp.logical_not(local))
        def _():
            rcopy(fsend.at[n], frecv.at[x], fs.at[n], fr.at[x], dev(z, to_x, y, n % 2)).start()

    for n in range(4):
        rcopy(fsend.at[n], frecv.at[n], fs.at[n], fr.at[n], other).wait_recv()
    mixed = frecv[...].reshape(896, 128)
    out_ref[...] = jnp.transpose(mixed, (1, 0))

    for n in range(4):
        to_x = (n // 2) * 2 + core

        @pl.when(jnp.logical_not(jnp.logical_and(to_x == x, core == n % 2)))
        def _():
            rcopy(fsend.at[n], frecv.at[n], fs.at[n], fr.at[n], other).wait_send()

    @pl.when(jnp.logical_not(at_home))
    def _():
        rcopy(wt, wbuf.at[wj, xl], w0.at[0], wr.at[wj, xl], other).wait_send()

    @pl.when(core == keeper)
    def _():
        for part in range(2):
            for n in range(2):
                slot = wbuf.at[wj, part]
                rcopy(slot, slot, ws.at[n, wj, part], wr.at[wj, part], other).wait_send()

    for s in range(1, 4):
        for up in (True, False):
            zsrc = lax.rem(z + (8 - s if up else s), 8)
            j = lax.rem(zsrc, 4)

            @pl.when(core == zsrc // 4)
            def _():
                far = 0 if up else 1
                n = 0 if up else 1
                for part, most in ((far, 4), (1 - far, 3)):
                    if s < most:
                        slot = wbuf.at[j, part]
                        rcopy(slot, slot, ws.at[n, j, part], wr.at[j, part], other).wait_send()


def body(queries, latent_rope, key_up, value_up, out_weight, plan):
    flat = plan.reshape(1, 64)
    ids = lax.broadcasted_iota(jnp.int32, (64, 64), 0)
    slots = lax.broadcasted_iota(jnp.int32, (64, 64), 1)
    inv = jnp.sum(jnp.where(flat == ids, slots, 0), axis=1)
    vm = pl.BlockSpec(memory_space=pltpu.VMEM)
    sm = pl.BlockSpec(memory_space=pltpu.SMEM)
    bf, f32 = jnp.bfloat16, jnp.float32
    dma = pltpu.SemaphoreType.DMA
    rows = GROUP * BLOCK
    return pl.pallas_call(
        kernel,
        out_shape=jax.ShapeDtypeStruct((128, 896), bf),
        in_specs=[sm, sm, vm, vm, vm, vm, vm],
        out_specs=vm,
        scratch_shapes=[
            pltpu.VMEM((8, 16, 32, WIDE), bf),
            pltpu.VMEM((2, 2, rows, WIDE), bf),
            pltpu.VMEM((TASKS, rows, 256), f32),
            pltpu.VMEM((TASKS + 1, rows, 128), f32),
            pltpu.VMEM((2, rows, 128), f32),
            pltpu.VMEM((TASKS + 1, rows, 128), f32),
            pltpu.VMEM((TASKS + 1, rows, LATENT), f32),
            pltpu.VMEM((224, 1024), bf),
            pltpu.VMEM((4, 2, 224, 1024), bf),
            pltpu.VMEM((2, 2, 2, 128, 1024), bf),
            pltpu.VMEM((4, 224, 512), bf),
            pltpu.VMEM((4, 224, 512), bf),
            pltpu.VMEM((4, 224, 128), bf),
            pltpu.VMEM((4, 224, 128), bf),
            dma((7,)), dma((7,)), dma((3,)), dma((3,)), dma((4, 2)), dma((4, 2)),
            dma((4, 2)), dma((4, 2)), dma((1,)), dma((2, 4, 2)), dma((4, 2)),
            dma((2, 3)), dma((2, 3)), dma((2, 4)), dma((2, 4)), dma((4,)), dma((4,)),
            dma((4,)), dma((4,)),
        ],
        compiler_params=pltpu.CompilerParams(
            collective_id=0, has_side_effects=True, vmem_limit_bytes=56 * 2**20
        ),
    )(plan, inv, queries, latent_rope, key_up, value_up, out_weight)


def solution(mesh):
    placed = (
        P("ctx", "head"),
        P("ctx", None),
        P(None, "head"),
        P(None, "head"),
        P("head", "ctx"),
        P(),
    )
    return jax.shard_map(
        body, mesh=mesh, in_specs=placed, out_specs=P("ctx", "head"), check_vma=False
    )
```

```python
import jax
import jax.numpy as jnp
from jax import lax
from jax.experimental import pallas as pl
from jax.experimental.pallas import tpu as pltpu
from jax.sharding import PartitionSpec as P

MESH = pl.DeviceIdType.MESH
NOPE = 128
ROPE = 64
VDIM = 128
LATENT = 512
HEAD_LOCAL = 8
BLOCK = 64
ROWS = HEAD_LOCAL * BLOCK
EARLY = 9
LATE = 8
WIDE = 640
PIECE = 144
NEG = -1e30
SCALE2 = 1.4426950408889634 * (NOPE + ROPE) ** -0.5


def nt(a, b):
    return lax.dot_general(a, b, (((1,), (1,)), ((), ())), preferred_element_type=jnp.float32)


def kernel(
    plan_ref, lrt_ref, q_hbm, ku_hbm, vu_hbm, w_hbm, out_ref,
    place, lat, qv, kuv, vuv, qs, sbuf, mrun, mfin, lrun, acc, wbuf, att, csend, crecv,
    ls, zs, zr, xs, xr, ys, yr, ks, kr, w0, ws, wr, as_, ar, bs, br, cs, cr,
):
    ctx = lax.axis_index("ctx")
    head = lax.axis_index("head")
    core = lax.rem(ctx, 2)
    xh = lax.rem(ctx // 2, 2)
    z = ctx // 4
    xl = head // 4
    y = lax.rem(head, 4)
    x = xh * 2 + xl

    def dev(z_, x_, y_, c_):
        return ((z_ * 2 + x_ // 2) * 2 + c_, lax.rem(x_, 2) * 4 + y_)

    def zdev(d):
        return dev(lax.rem(z + d, 8), x, y, core)

    def xdev(o):
        return dev(z, lax.rem(x + o, 4), y, core)

    def ydev(o):
        return dev(z, x, lax.rem(y + o, 4), core)

    other = dev(z, x, y, 1 - core)

    def rcopy(src, dst, ssem, rsem, target):
        return pltpu.make_async_remote_copy(
            src_ref=src, dst_ref=dst, send_sem=ssem, recv_sem=rsem,
            device_id=target, device_id_type=MESH,
        )

    barrier = pltpu.get_barrier_semaphore()
    for d in range(1, 8):
        pl.semaphore_signal(barrier, 1, device_id=zdev(d), device_id_type=MESH)
    for oy in range(4):
        for ox in range(4):
            for oc in range(2):
                if oy or ox or oc:
                    pl.semaphore_signal(
                        barrier, 1,
                        device_id=dev(z, lax.rem(x + ox, 4), lax.rem(y + oy, 4), lax.rem(core + oc, 2)),
                        device_id_type=MESH,
                    )
    loads = [
        pltpu.make_async_copy(q_hbm, qv, ls.at[0]),
        pltpu.make_async_copy(ku_hbm, kuv, ls.at[1]),
        pltpu.make_async_copy(vu_hbm, vuv, ls.at[2]),
    ]
    for cp in loads:
        cp.start()

    def place_of(b, carry):
        found = jnp.int32(0)
        for c in range(32):
            found = jnp.where(jnp.minimum(plan_ref[0, c], plan_ref[1, c]) == b, c, found)
        place[b] = found
        return carry

    lax.fori_loop(0, 32, place_of, 0)

    par = lax.rem(y, 2)

    def piece(src_x, parity, c_):
        return (src_x // 2) * 8 + c_ * 4 + parity * 2 + lax.rem(src_x, 2)

    mine = piece(x, par, core)
    rows_all = jnp.transpose(lrt_ref[...], (1, 0))
    quarter = par * 2 + xl
    for q in range(4):
        @pl.when(quarter == q)
        def _():
            part = rows_all[q * 32 : (q + 1) * 32]
            for c in range(4):
                lat[z, mine, c * 32 : (c + 1) * 32] = part[:, c * 128 : (c + 1) * 128]
            rope = part[:, LATENT:]
            lat[z, mine, 128:PIECE] = jnp.concatenate([rope[:16], rope[16:]], axis=1)

    def dist(i):
        if isinstance(i, int):
            return 0
        return lax.rem(jnp.where(lax.rem(i, 2) == 1, (i + 1) // 2, 8 - i // 2), 8)

    def source(i):
        return lax.rem(z + 8 - dist(i), 8)

    def spread(o, i, zsrc, idx):
        slot = lat.at[zsrc, idx]
        to = lax.rem(y + 1 + 2 * (i % 2), 4)
        rcopy(slot, slot, ys.at[o, i], yr.at[o, i], dev(z, x, to, core)).start()
        rcopy(slot, slot, ks.at[o, i], kr.at[o, i], other).start()

    pair = x + 1 - 2 * xl
    cross = 3 - x
    origin = (x, pair, cross, lax.rem(x + 2, 4))

    def from_z(i):
        zsrc = source(i)
        slot = lat.at[zsrc, mine]
        d = dist(i)

        if not isinstance(i, int):
            rcopy(slot, slot, zs.at[d], zr.at[d], other).wait_recv()
        rcopy(slot, slot, xs.at[1, i], xr.at[1, i], dev(z, pair, y, core)).start()
        rcopy(slot, slot, xs.at[2, i], xr.at[2, i], dev(z, cross, y, core)).start()
        spread(0, i, zsrc, mine)

    def from_x(i, o):
        zsrc = source(i)
        idx = piece(origin[o], par, core)
        slot = lat.at[zsrc, idx]
        rcopy(slot, slot, xs.at[o, i], xr.at[o, i], other).wait_recv()
        if o == 1:
            rcopy(slot, slot, xs.at[3, i], xr.at[3, i], dev(z, cross, y, core)).start()
        spread(o, i, zsrc, idx)

    def from_y(i):
        zsrc = source(i)
        for o in range(4):
            idx = piece(origin[o], 1 - par, core)
            slot = lat.at[zsrc, idx]
            rcopy(slot, slot, ys.at[o, i], yr.at[o, i], other).wait_recv()
            rcopy(slot, slot, ks.at[4 + o, i], kr.at[4 + o, i], other).start()

    def stage(m, carry):
        @pl.when(m < 4)
        def _():
            from_z(2 * m + 1)

        @pl.when(m < 3)
        def _():
            from_z(2 * m + 2)

        @pl.when(m < 8)
        def _():
            from_x(m, 1)
            from_x(m, 2)

        @pl.when(jnp.logical_and(m >= 1, m < 9))
        def _():
            from_x(m - 1, 3)

        @pl.when(m >= 3)
        def _():
            from_y(m - 3)

        return carry

    pl.semaphore_wait(barrier, 38)

    for d in (1, 7, 2, 6, 3, 5, 4):
        rcopy(lat.at[z, mine], lat.at[z, mine], zs.at[d], zr.at[d], zdev(d)).start()

    from_z(0)

    wj = lax.rem(z, 4)
    keeper = z // 4
    at_home = jnp.logical_and(core == xl, core == keeper)

    @pl.when(at_home)
    def _():
        pltpu.make_async_copy(w_hbm, wbuf.at[wj, xl], wr.at[wj, xl]).start()

    @pl.when(jnp.logical_not(at_home))
    def _():
        rcopy(
            w_hbm, wbuf.at[wj, xl], w0.at[0], wr.at[wj, xl], dev(z, xh * 2 + core, y, keeper)
        ).start()

    for cp in loads:
        cp.wait()
    for h in range(HEAD_LOCAL):
        lo = h * (NOPE + ROPE)
        qn = qv[:, lo : lo + NOPE]
        qr = qv[:, lo + NOPE : lo + NOPE + ROPE].astype(jnp.float32) * SCALE2
        qr = qr.astype(jnp.bfloat16)
        ql = (nt(qn, kuv[:, h * NOPE : (h + 1) * NOPE]) * SCALE2).astype(jnp.bfloat16)
        qr = jnp.concatenate([qr, qr], axis=1)
        for i in range(2):
            qs[i, h * BLOCK : (h + 1) * BLOCK, 0:LATENT] = ql[i * BLOCK : (i + 1) * BLOCK]
            qs[i, h * BLOCK : (h + 1) * BLOCK, LATENT:WIDE] = qr[i * BLOCK : (i + 1) * BLOCK]

    def ring_send(j, part, up):
        slot = wbuf.at[j, part]
        n = 0 if up else 1
        rcopy(slot, slot, ws.at[n, j, part], wr.at[j, part], zdev(1 if up else 7)).start()

    def ring_wait(j, part):
        slot = wbuf.at[j, part]
        rcopy(slot, slot, w0.at[0], wr.at[j, part], other).wait_recv()

    def ring_step(s):
        if s == 0:
            @pl.when(core == keeper)
            def _():
                for part in range(2):
                    ring_wait(wj, part)
                for part in range(2):
                    ring_send(wj, part, True)
                    ring_send(wj, part, False)
            return
        for up in (True, False):
            zsrc = lax.rem(z + (8 - s if up else s), 8)
            j = lax.rem(zsrc, 4)

            @pl.when(core == zsrc // 4)
            def _():
                far = 0 if up else 1
                if s <= 4:
                    ring_wait(j, far)
                if s <= 3:
                    ring_wait(j, 1 - far)
                if s < 4:
                    ring_send(j, far, up)
                if s < 3:
                    ring_send(j, 1 - far, up)

    lax.fori_loop(0, 2, stage, 0)
    ring_step(0)
    lax.fori_loop(2, 8, stage, 0)
    ring_step(1)
    lax.fori_loop(8, 11, stage, 0)

    def core_wait(i, carry):
        zsrc = source(i)
        for o in range(4):
            for n, parity in ((0, par), (4, 1 - par)):
                slot = lat.at[zsrc, piece(origin[o], parity, 1 - core)]
                rcopy(slot, slot, ks.at[n + o, i], kr.at[n + o, i], other).wait_recv()
        return carry

    lax.fori_loop(0, 8, core_wait, 0)

    p0 = plan_ref[0, ctx]
    p1 = plan_ref[1, ctx]
    low = jnp.minimum(p0, p1)
    high = jnp.maximum(p0, p1)
    low_at = jnp.where(p0 < p1, 0, 1)
    beta = lax.div(low, 4)
    row_of = lax.broadcasted_iota(jnp.int32, (ROWS, 256), 0) % BLOCK
    ahead = lax.broadcasted_iota(jnp.int32, (ROWS, 256), 1) - row_of
    left = lax.broadcasted_iota(jnp.int32, (16, 128), 1) < 64
    none = jnp.zeros((16, 128), jnp.bfloat16)

    def chunk_of(t):
        return jnp.where(t <= beta, t, t - beta - 1)

    def pieces_of(t):
        first = chunk_of(t) * 4
        got = []
        for i in range(4):
            c = place[jnp.minimum(first + i, 63 - first - i)]
            s = 2 * c + jnp.where(plan_ref[0, c] == first + i, 0, 1)
            pair = lat[lax.div(s, 8), pl.ds(lax.rem(s, 8) * 2, 2)]
            got += [pair[0], pair[1]]
        return got

    def wide_of(got):
        return jnp.concatenate(
            [
                jnp.concatenate([p[c * 32 : (c + 1) * 32] for p in got], axis=0)
                for c in range(4)
            ],
            axis=1,
        )

    def keys_of(t):
        got = pieces_of(t)
        rope = []
        for p in got:
            r = p[128:PIECE]
            rope += [jnp.where(left, r, none), jnp.where(left, none, r)]
        return jnp.concatenate([wide_of(got), jnp.concatenate(rope, axis=0)], axis=1)

    def values_of(t):
        return wide_of(pieces_of(t))

    def fold(s):
        return jnp.maximum(s[:, :128], s[:, 128:])

    mrun[0] = jnp.full((ROWS, 128), NEG, jnp.float32)
    lrun[0] = jnp.zeros((ROWS, 128), jnp.float32)
    acc[0] = jnp.zeros((ROWS, LATENT), jnp.float32)

    def score(t, carry):
        is_low = t <= beta
        q = qs[jnp.where(is_low, low_at, 1 - low_at)]
        s = nt(q, keys_of(t))
        room = jnp.where(is_low, low, high) * BLOCK - chunk_of(t) * 256
        s = jnp.where(ahead <= room, s, NEG)
        sbuf[t] = s
        before = jnp.where(t == beta + 1, NEG, mrun[t])
        mrun[t + 1] = jnp.maximum(before, fold(s))
        return carry

    def row_max(at):
        return jnp.broadcast_to(jnp.max(mrun[at], axis=1, keepdims=True), (ROWS, 128))

    def weights(s, m):
        wa = jnp.exp2(s[:, :128] - m)
        wb = jnp.exp2(s[:, 128:] - m)
        return wa + wb, jnp.concatenate([wa, wb], axis=1).astype(jnp.bfloat16)

    def weigh(t, carry):
        is_low = t <= beta
        keep = jnp.where(t == beta + 1, 0.0, 1.0)
        total, w = weights(sbuf[t], mfin[jnp.where(is_low, 0, 1)])
        lrun[t + 1] = lrun[t] * keep + total
        added = jnp.dot(w, values_of(t), preferred_element_type=jnp.float32)
        acc[t + 1] = acc[t] * keep + added
        return carry

    def normal(at):
        total = jnp.sum(lrun[at], axis=1, keepdims=True)
        return (acc[at] / total).astype(jnp.bfloat16)

    def shard(half, src_x, c_):
        return att.at[half, lax.rem(src_x, 2), src_x // 2, c_]

    def finish(half, o):
        for h in range(HEAD_LOCAL):
            up = jnp.dot(
                o[h * BLOCK : (h + 1) * BLOCK],
                vuv[:, h * VDIM : (h + 1) * VDIM],
                preferred_element_type=jnp.float32,
            )
            att[half, xl, xh, core, :, h * VDIM : (h + 1) * VDIM] = up.astype(jnp.bfloat16)
        here = shard(half, x, core)
        for n in (1, 3, 2):
            rcopy(here, here, as_.at[half, n], ar.at[half, n], xdev(n)).start()
        rcopy(here, here, bs.at[half, 0], br.at[half, 0], other).start()

    def pass_on(half):
        for n in (1, 3, 2):
            there = shard(half, lax.rem(x + 4 - n, 4), core)
            rcopy(there, there, as_.at[half, n], ar.at[half, n], other).wait_recv()
            rcopy(there, there, bs.at[half, n], br.at[half, n], other).start()

    def gathered(half):
        for n in range(4):
            there = shard(half, lax.rem(x + 4 - n, 4), 1 - core)
            rcopy(there, there, bs.at[half, n], br.at[half, n], other).wait_recv()

    lax.fori_loop(0, EARLY, score, 0)
    mfin[0] = row_max(beta + 1)
    mfin[1] = row_max(EARLY)
    ring_step(2)
    lax.fori_loop(0, EARLY, weigh, 0)
    finish(0, normal(beta + 1))

    def late_score(i, carry):
        t = EARLY + i
        s = nt(qs[1 - low_at], keys_of(t))
        room = high * BLOCK - chunk_of(t) * 256
        s = jnp.where(ahead <= room, s, NEG)
        sbuf[i] = s
        mrun[t + 1] = jnp.maximum(mrun[t], fold(s))
        return carry

    lax.fori_loop(0, LATE, late_score, 0)
    mfin[0] = row_max(EARLY + LATE)
    again = jnp.exp2(mfin[1] - mfin[0])
    lrun[EARLY] = lrun[EARLY] * again
    acc[EARLY] = acc[EARLY] * jnp.concatenate([again] * 4, axis=1)
    pass_on(0)

    def late_weigh(i, carry):
        m = mfin[0]
        total, w = weights(sbuf[2 * i], m)
        total2, w2 = weights(sbuf[2 * i + 1], m)
        lrun[EARLY] = lrun[EARLY] + (total + total2)
        v = jnp.concatenate([values_of(EARLY + 2 * i), values_of(EARLY + 2 * i + 1)], axis=0)
        acc[EARLY] = acc[EARLY] + jnp.dot(
            jnp.concatenate([w, w2], axis=1), v, preferred_element_type=jnp.float32
        )
        return carry

    lax.fori_loop(0, LATE // 2, late_weigh, 0)
    finish(1, normal(EARLY))

    def project(half, zsrc):
        j = lax.rem(zsrc, 4)

        @pl.when(core == zsrc // 4)
        def _():
            total = nt(wbuf[j, 0], att[half, 0].reshape(256, 1024)) + nt(
                wbuf[j, 1], att[half, 1].reshape(256, 1024)
            )
            total = total.astype(jnp.bfloat16)
            for n in range(4):
                lanes = total[:, n * BLOCK : (n + 1) * BLOCK]
                csend[half, j, n] = jnp.concatenate([lanes[:112], lanes[112:]], axis=1)
            for n in range(4):
                to_x = (n // 2) * 2 + core
                local = jnp.logical_and(jnp.logical_and(to_x == x, core == n % 2), j == y)

                @pl.when(local)
                def _():
                    pltpu.make_async_copy(
                        csend.at[half, j, n], crecv.at[half, y, x], cr.at[half, y, x]
                    ).start()

                @pl.when(jnp.logical_not(local))
                def _():
                    rcopy(
                        csend.at[half, j, n], crecv.at[half, y, x], cs.at[half, j, n],
                        cr.at[half, y, x], dev(z, to_x, j, n % 2),
                    ).start()

    def both(half, s):
        project(half, lax.rem(z + 8 - s, 8))
        project(half, lax.rem(z + s, 8))

    def near(half):
        def loop(s, carry):
            both(half, s)
            return carry

        project(half, z)
        lax.fori_loop(1, 3, loop, 0)

    ring_step(3)
    gathered(0)
    near(0)
    both(0, 3)
    ring_step(4)
    project(0, lax.rem(z + 4, 8))
    pass_on(1)
    gathered(1)
    near(1)
    both(1, 3)
    project(1, lax.rem(z + 4, 8))

    halves = []
    for half in range(2):
        columns = []
        for n in range(4):
            total = None
            for m in range(4):
                slot = crecv.at[half, m, n]
                rcopy(slot, slot, cs.at[half, m, n], cr.at[half, m, n], other).wait_recv()
                term = slot[...].astype(jnp.float32)
                total = term if total is None else total + term
            columns += [total[:, :BLOCK], total[:, BLOCK:]]
        halves.append(jnp.concatenate(columns, axis=0))
    first = jnp.where(low_at == 0, halves[0], halves[1])
    second = jnp.where(low_at == 0, halves[1], halves[0])
    mixed = jnp.concatenate([first, second], axis=1)
    out_ref[...] = jnp.transpose(mixed, (1, 0)).astype(jnp.bfloat16)

    for d in range(1, 8):
        slot = lat.at[z, mine]
        rcopy(slot, slot, zs.at[d], zr.at[d], other).wait_send()

    def left_core(i, carry):
        slot = lat.at[z, mine]
        for o in range(4):
            if o:
                rcopy(slot, slot, xs.at[o, i], xr.at[o, i], other).wait_send()
            rcopy(slot, slot, ys.at[o, i], yr.at[o, i], other).wait_send()
            rcopy(slot, slot, ks.at[o, i], kr.at[o, i], other).wait_send()
            rcopy(slot, slot, ks.at[4 + o, i], kr.at[4 + o, i], other).wait_send()
        return carry

    lax.fori_loop(0, 8, left_core, 0)
    for half in range(2):
        here = shard(half, x, core)
        for n in range(4):
            if n:
                rcopy(here, here, as_.at[half, n], ar.at[half, n], other).wait_send()
            rcopy(here, here, bs.at[half, n], br.at[half, n], other).wait_send()
        for j in range(4):
            for n in range(4):
                to_x = (n // 2) * 2 + core
                local = jnp.logical_and(jnp.logical_and(to_x == x, core == n % 2), j == y)

                @pl.when(jnp.logical_not(local))
                def _():
                    slot = csend.at[half, j, n]
                    rcopy(slot, slot, cs.at[half, j, n], cr.at[half, j, n], other).wait_send()

    @pl.when(jnp.logical_not(at_home))
    def _():
        rcopy(w_hbm, wbuf.at[wj, xl], w0.at[0], wr.at[wj, xl], other).wait_send()

    @pl.when(core == keeper)
    def _():
        for part in range(2):
            for n in range(2):
                slot = wbuf.at[wj, part]
                rcopy(slot, slot, ws.at[n, wj, part], wr.at[wj, part], other).wait_send()

    for s in range(1, 4):
        for up in (True, False):
            zsrc = lax.rem(z + (8 - s if up else s), 8)
            j = lax.rem(zsrc, 4)

            @pl.when(core == zsrc // 4)
            def _():
                far = 0 if up else 1
                n = 0 if up else 1
                for part, most in ((far, 4), (1 - far, 3)):
                    if s < most:
                        slot = wbuf.at[j, part]
                        rcopy(slot, slot, ws.at[n, j, part], wr.at[j, part], other).wait_send()


def body(queries, latent_rope, key_up, value_up, out_weight, plan):
    vm = pl.BlockSpec(memory_space=pltpu.VMEM)
    sm = pl.BlockSpec(memory_space=pltpu.SMEM)
    anywhere = pl.BlockSpec(memory_space=pl.ANY)
    bf, f32 = jnp.bfloat16, jnp.float32
    dma = pltpu.SemaphoreType.DMA
    return pl.pallas_call(
        kernel,
        out_shape=jax.ShapeDtypeStruct((128, 896), bf),
        in_specs=[sm, vm, anywhere, anywhere, anywhere, anywhere],
        out_specs=vm,
        scratch_shapes=[
            pltpu.SMEM((32,), jnp.int32),
            pltpu.VMEM((8, 16, PIECE, 128), bf),
            pltpu.VMEM((128, 1536), bf),
            pltpu.VMEM((512, 1024), bf),
            pltpu.VMEM((512, 1024), bf),
            pltpu.VMEM((2, ROWS, WIDE), bf),
            pltpu.VMEM((EARLY, ROWS, 256), f32),
            pltpu.VMEM((EARLY + LATE + 1, ROWS, 128), f32),
            pltpu.VMEM((2, ROWS, 128), f32),
            pltpu.VMEM((EARLY + 1, ROWS, 128), f32),
            pltpu.VMEM((EARLY + 1, ROWS, LATENT), f32),
            pltpu.VMEM((4, 2, 224, 1024), bf),
            pltpu.VMEM((2, 2, 2, 2, BLOCK, 1024), bf),
            pltpu.VMEM((2, 4, 4, 112, 128), bf),
            pltpu.VMEM((2, 4, 4, 112, 128), bf),
            dma((3,)), dma((8,)), dma((8,)), dma((4, 8)), dma((4, 8)), dma((4, 8)), dma((4, 8)),
            dma((8, 8)), dma((8, 8)), dma((1,)), dma((2, 4, 2)), dma((4, 2)),
            dma((2, 4)), dma((2, 4)), dma((2, 4)), dma((2, 4)), dma((2, 4, 4)), dma((2, 4, 4)),
        ],
        compiler_params=pltpu.CompilerParams(
            collective_id=0, has_side_effects=True, vmem_limit_bytes=56 * 2**20
        ),
    )(plan.T, latent_rope.T, queries, key_up, value_up, out_weight.T)


def solution(mesh):
    placed = (
        P("ctx", "head"),
        P("ctx", None),
        P(None, "head"),
        P(None, "head"),
        P("head", "ctx"),
        P(),
    )
    return jax.shard_map(
        body, mesh=mesh, in_specs=placed, out_specs=P("ctx", "head"), check_vma=False
    )
```

```python
import jax
import jax.numpy as jnp
from jax import lax
from jax.experimental import pallas as pl
from jax.experimental.pallas import tpu as pltpu
from jax.sharding import PartitionSpec as P

MESH = pl.DeviceIdType.MESH
NOPE = 128
ROPE = 64
VDIM = 128
LATENT = 512
HEAD_LOCAL = 8
BLOCK = 64
ROWS = HEAD_LOCAL * BLOCK
EARLY = 9
LATE = 8
WIDE = 640
PIECE = 144
NEG = -1e30
SCALE2 = 1.4426950408889634 * (NOPE + ROPE) ** -0.5


def nt(a, b):
    return lax.dot_general(a, b, (((1,), (1,)), ((), ())), preferred_element_type=jnp.float32)


def kernel(
    plan_ref, lrt_hbm, q_hbm, ku_hbm, vu_hbm, w_hbm, out_ref,
    place, lrt, lat, qv, kuv, vuv, qs, sbuf, mrun, mfin, lrun, acc, wbuf, att, csend, crecv,
    ls, zs, zr, xs, xr, ys, yr, ks, kr, w0, ws, wr, as_, ar, bs, br, cs, cr,
):
    ctx = lax.axis_index("ctx")
    head = lax.axis_index("head")
    core = lax.rem(ctx, 2)
    xh = lax.rem(ctx // 2, 2)
    z = ctx // 4
    xl = head // 4
    y = lax.rem(head, 4)
    x = xh * 2 + xl

    def dev(z_, x_, y_, c_):
        return ((z_ * 2 + x_ // 2) * 2 + c_, lax.rem(x_, 2) * 4 + y_)

    def zdev(d):
        return dev(lax.rem(z + d, 8), x, y, core)

    def xdev(o):
        return dev(z, lax.rem(x + o, 4), y, core)

    def ydev(o):
        return dev(z, x, lax.rem(y + o, 4), core)

    other = dev(z, x, y, 1 - core)

    def rcopy(src, dst, ssem, rsem, target):
        return pltpu.make_async_remote_copy(
            src_ref=src, dst_ref=dst, send_sem=ssem, recv_sem=rsem,
            device_id=target, device_id_type=MESH,
        )

    loads = [
        pltpu.make_async_copy(lrt_hbm, lrt, ls.at[3]),
        pltpu.make_async_copy(q_hbm, qv, ls.at[0]),
        pltpu.make_async_copy(ku_hbm, kuv, ls.at[1]),
        pltpu.make_async_copy(vu_hbm, vuv, ls.at[2]),
    ]
    for cp in loads:
        cp.start()

    barrier = pltpu.get_barrier_semaphore()
    for d in range(1, 8):
        pl.semaphore_signal(barrier, 1, device_id=zdev(d), device_id_type=MESH)
    for oy in range(4):
        for ox in range(4):
            for oc in range(2):
                if oy or ox or oc:
                    pl.semaphore_signal(
                        barrier, 1,
                        device_id=dev(z, lax.rem(x + ox, 4), lax.rem(y + oy, 4), lax.rem(core + oc, 2)),
                        device_id_type=MESH,
                    )
    par = lax.rem(y, 2)

    def piece(src_x, parity, c_):
        return (src_x // 2) * 8 + c_ * 4 + parity * 2 + lax.rem(src_x, 2)

    mine = piece(x, par, core)
    loads[0].wait()
    rows_all = jnp.transpose(lrt[...], (1, 0))
    quarter = par * 2 + xl
    for q in range(4):
        @pl.when(quarter == q)
        def _():
            part = rows_all[q * 32 : (q + 1) * 32]
            for c in range(4):
                lat[z, mine, c * 32 : (c + 1) * 32] = part[:, c * 128 : (c + 1) * 128]
            rope = part[:, LATENT:]
            lat[z, mine, 128:PIECE] = jnp.concatenate([rope[:16], rope[16:]], axis=1)

    def dist(i):
        if isinstance(i, int):
            return 0
        return lax.rem(jnp.where(lax.rem(i, 2) == 1, (i + 1) // 2, 8 - i // 2), 8)

    def source(i):
        return lax.rem(z + 8 - dist(i), 8)

    def spread(o, i, zsrc, idx):
        slot = lat.at[zsrc, idx]
        to = lax.rem(y + 1 + 2 * (i % 2), 4)
        rcopy(slot, slot, ys.at[0], yr.at[o, i], dev(z, x, to, core)).start()
        rcopy(slot, slot, ks.at[0], kr.at[0], other).start()

    pair = x + 1 - 2 * xl
    cross = 3 - x
    origin = (x, pair, cross, lax.rem(x + 2, 4))

    def from_z(i):
        zsrc = source(i)
        slot = lat.at[zsrc, mine]
        d = dist(i)

        if not isinstance(i, int):
            rcopy(slot, slot, zs.at[0], zr.at[d], other).wait_recv()
        rcopy(slot, slot, xs.at[0], xr.at[1, i], dev(z, pair, y, core)).start()
        rcopy(slot, slot, xs.at[0], xr.at[2, i], dev(z, cross, y, core)).start()
        spread(0, i, zsrc, mine)

    def from_x(i, o):
        zsrc = source(i)
        idx = piece(origin[o], par, core)
        slot = lat.at[zsrc, idx]
        rcopy(slot, slot, xs.at[0], xr.at[o, i], other).wait_recv()
        if o == 1:
            rcopy(slot, slot, xs.at[0], xr.at[3, i], dev(z, cross, y, core)).start()
        spread(o, i, zsrc, idx)

    def from_y(i):
        zsrc = source(i)
        for o in range(4):
            idx = piece(origin[o], 1 - par, core)
            slot = lat.at[zsrc, idx]
            rcopy(slot, slot, ys.at[0], yr.at[o, i], other).wait_recv()
            rcopy(slot, slot, ks.at[0], kr.at[0], other).start()

    def stage(m, carry):
        @pl.when(m < 4)
        def _():
            from_z(2 * m + 1)

        @pl.when(m < 3)
        def _():
            from_z(2 * m + 2)

        @pl.when(m < 8)
        def _():
            from_x(m, 1)
            from_x(m, 2)

        @pl.when(jnp.logical_and(m >= 1, m < 9))
        def _():
            from_x(m - 1, 3)

        @pl.when(m >= 3)
        def _():
            from_y(m - 3)

        return carry

    pl.semaphore_wait(barrier, 38)

    for d in (1, 7, 2, 6, 3, 5, 4):
        rcopy(lat.at[z, mine], lat.at[z, mine], zs.at[0], zr.at[d], zdev(d)).start()

    from_z(0)

    wj = lax.rem(z, 4)
    keeper = z // 4
    at_home = jnp.logical_and(core == xl, core == keeper)

    @pl.when(at_home)
    def _():
        pltpu.make_async_copy(w_hbm, wbuf.at[wj, xl], wr.at[wj, xl]).start()

    @pl.when(jnp.logical_not(at_home))
    def _():
        rcopy(
            w_hbm, wbuf.at[wj, xl], w0.at[0], wr.at[wj, xl], dev(z, xh * 2 + core, y, keeper)
        ).start()

    def place_of(b, carry):
        found = jnp.int32(0)
        for c in range(32):
            found = jnp.where(jnp.minimum(plan_ref[0, c], plan_ref[1, c]) == b, c, found)
        place[b] = found
        return carry

    lax.fori_loop(0, 32, place_of, 0)

    for cp in loads[1:]:
        cp.wait()
    for h in range(HEAD_LOCAL):
        lo = h * (NOPE + ROPE)
        qn = qv[:, lo : lo + NOPE]
        qr = qv[:, lo + NOPE : lo + NOPE + ROPE].astype(jnp.float32) * SCALE2
        qr = qr.astype(jnp.bfloat16)
        ql = (nt(qn, kuv[:, h * NOPE : (h + 1) * NOPE]) * SCALE2).astype(jnp.bfloat16)
        qr = jnp.concatenate([qr, qr], axis=1)
        for i in range(2):
            qs[i, h * BLOCK : (h + 1) * BLOCK, 0:LATENT] = ql[i * BLOCK : (i + 1) * BLOCK]
            qs[i, h * BLOCK : (h + 1) * BLOCK, LATENT:WIDE] = qr[i * BLOCK : (i + 1) * BLOCK]

    def ring_send(j, part, up):
        slot = wbuf.at[j, part]
        n = 0 if up else 1
        rcopy(slot, slot, ws.at[n, j, part], wr.at[j, part], zdev(1 if up else 7)).start()

    def ring_wait(j, part):
        slot = wbuf.at[j, part]
        rcopy(slot, slot, w0.at[0], wr.at[j, part], other).wait_recv()

    def ring_moves(s, q):
        part = xl if q == 0 else 1 - xl
        for up in (True, False):
            reach = jnp.where((part == 0) == up, 4, 3)
            yield up, part, lax.rem(z + (8 - s if up else s), 8), reach

    def ring_step(s, q):
        if s == 0:
            part = xl if q == 0 else 1 - xl

            @pl.when(core == keeper)
            def _():
                ring_wait(wj, part)
                ring_send(wj, part, True)
                ring_send(wj, part, False)
            return
        for up, part, zsrc, reach in ring_moves(s, q):
            j = lax.rem(zsrc, 4)

            @pl.when(jnp.logical_and(core == zsrc // 4, s <= reach))
            def _():
                ring_wait(j, part)

            @pl.when(jnp.logical_and(core == zsrc // 4, s < reach))
            def _():
                ring_send(j, part, up)

    ring_step(0, 0)
    lax.fori_loop(0, 2, stage, 0)
    ring_step(0, 1)
    lax.fori_loop(2, 3, stage, 0)
    ring_step(1, 0)
    lax.fori_loop(3, 6, stage, 0)
    ring_step(1, 1)
    lax.fori_loop(6, 9, stage, 0)
    ring_step(2, 0)
    lax.fori_loop(9, 11, stage, 0)

    many = lat.at[pl.ds(0, 4)]
    rcopy(many, many, ks.at[0], kr.at[0], other).wait_recv()
    ring_step(2, 1)

    p0 = plan_ref[0, ctx]
    p1 = plan_ref[1, ctx]
    low = jnp.minimum(p0, p1)
    high = jnp.maximum(p0, p1)
    low_at = jnp.where(p0 < p1, 0, 1)
    beta = lax.div(low, 4)
    row_of = lax.broadcasted_iota(jnp.int32, (ROWS, 256), 0) % BLOCK
    ahead = lax.broadcasted_iota(jnp.int32, (ROWS, 256), 1) - row_of
    left = lax.broadcasted_iota(jnp.int32, (16, 128), 1) < 64
    none = jnp.zeros((16, 128), jnp.bfloat16)

    def chunk_of(t):
        return jnp.where(t <= beta, t, t - beta - 1)

    def pieces_of(t):
        first = chunk_of(t) * 4
        got = []
        for i in range(4):
            c = place[jnp.minimum(first + i, 63 - first - i)]
            s = 2 * c + jnp.where(plan_ref[0, c] == first + i, 0, 1)
            pair = lat[lax.div(s, 8), pl.ds(lax.rem(s, 8) * 2, 2)]
            got += [pair[0], pair[1]]
        return got

    def wide_of(got):
        return jnp.concatenate(
            [
                jnp.concatenate([p[c * 32 : (c + 1) * 32] for p in got], axis=0)
                for c in range(4)
            ],
            axis=1,
        )

    def keys_of(t):
        got = pieces_of(t)
        rope = []
        for p in got:
            r = p[128:PIECE]
            rope += [jnp.where(left, r, none), jnp.where(left, none, r)]
        return jnp.concatenate([wide_of(got), jnp.concatenate(rope, axis=0)], axis=1)

    def values_of(t):
        return wide_of(pieces_of(t))

    def fold(s):
        return jnp.maximum(s[:, :128], s[:, 128:])

    mrun[0] = jnp.full((ROWS, 128), NEG, jnp.float32)
    lrun[0] = jnp.zeros((ROWS, 128), jnp.float32)
    acc[0] = jnp.zeros((ROWS, LATENT), jnp.float32)

    def score(t, carry):
        is_low = t <= beta
        q = qs[jnp.where(is_low, low_at, 1 - low_at)]
        s = nt(q, keys_of(t))
        room = jnp.where(is_low, low, high) * BLOCK - chunk_of(t) * 256
        s = jnp.where(ahead <= room, s, NEG)
        sbuf[t] = s
        before = jnp.where(t == beta + 1, NEG, mrun[t])
        mrun[t + 1] = jnp.maximum(before, fold(s))
        return carry

    def row_max(at):
        return jnp.broadcast_to(jnp.max(mrun[at], axis=1, keepdims=True), (ROWS, 128))

    def weights(s, m):
        wa = jnp.exp2(s[:, :128] - m)
        wb = jnp.exp2(s[:, 128:] - m)
        return wa + wb, jnp.concatenate([wa, wb], axis=1).astype(jnp.bfloat16)

    def weigh(t, carry):
        is_low = t <= beta
        keep = jnp.where(t == beta + 1, 0.0, 1.0)
        total, w = weights(sbuf[t], mfin[jnp.where(is_low, 0, 1)])
        lrun[t + 1] = lrun[t] * keep + total
        added = jnp.dot(w, values_of(t), preferred_element_type=jnp.float32)
        acc[t + 1] = acc[t] * keep + added
        return carry

    def normal(at):
        total = jnp.sum(lrun[at], axis=1, keepdims=True)
        return (acc[at] / total).astype(jnp.bfloat16)

    def shard(half, src_x, c_):
        return att.at[half, lax.rem(src_x, 2), src_x // 2, c_]

    def finish(half, o):
        for h in range(HEAD_LOCAL):
            up = jnp.dot(
                o[h * BLOCK : (h + 1) * BLOCK],
                vuv[:, h * VDIM : (h + 1) * VDIM],
                preferred_element_type=jnp.float32,
            )
            att[half, xl, xh, core, :, h * VDIM : (h + 1) * VDIM] = up.astype(jnp.bfloat16)
        here = shard(half, x, core)
        for n in (1, 3, 2):
            rcopy(here, here, as_.at[half, n], ar.at[half, n], xdev(n)).start()
        rcopy(here, here, bs.at[half, 0], br.at[half, 0], other).start()

    def pass_on(half):
        for n in (1, 3, 2):
            there = shard(half, lax.rem(x + 4 - n, 4), core)
            rcopy(there, there, as_.at[half, n], ar.at[half, n], other).wait_recv()
            rcopy(there, there, bs.at[half, n], br.at[half, n], other).start()

    def gathered(half):
        for n in range(4):
            there = shard(half, lax.rem(x + 4 - n, 4), 1 - core)
            rcopy(there, there, bs.at[half, n], br.at[half, n], other).wait_recv()

    lax.fori_loop(0, EARLY, score, 0, unroll=3)
    mfin[0] = row_max(beta + 1)
    mfin[1] = row_max(EARLY)
    lax.fori_loop(0, EARLY, weigh, 0, unroll=3)
    finish(0, normal(beta + 1))
    ring_step(3, 0)

    def late_score(i, carry):
        t = EARLY + i
        s = nt(qs[1 - low_at], keys_of(t))
        room = high * BLOCK - chunk_of(t) * 256
        s = jnp.where(ahead <= room, s, NEG)
        sbuf[i] = s
        mrun[t + 1] = jnp.maximum(mrun[t], fold(s))
        return carry

    lax.fori_loop(0, LATE, late_score, 0, unroll=2)
    mfin[0] = row_max(EARLY + LATE)
    again = jnp.exp2(mfin[1] - mfin[0])
    lrun[EARLY] = lrun[EARLY] * again
    acc[EARLY] = acc[EARLY] * jnp.concatenate([again] * 4, axis=1)
    ring_step(3, 1)

    def late_weigh(i, carry):
        m = mfin[0]
        total, w = weights(sbuf[2 * i], m)
        total2, w2 = weights(sbuf[2 * i + 1], m)
        lrun[EARLY] = lrun[EARLY] + (total + total2)
        v = jnp.concatenate([values_of(EARLY + 2 * i), values_of(EARLY + 2 * i + 1)], axis=0)
        acc[EARLY] = acc[EARLY] + jnp.dot(
            jnp.concatenate([w, w2], axis=1), v, preferred_element_type=jnp.float32
        )
        return carry

    lax.fori_loop(0, LATE // 2, late_weigh, 0, unroll=2)
    finish(1, normal(EARLY))
    pass_on(0)
    ring_step(4, 0)

    def product(half, j):
        if True:
            total = nt(wbuf[j, 0], att[half, 0].reshape(256, 1024)) + nt(
                wbuf[j, 1], att[half, 1].reshape(256, 1024)
            )
            total = total.astype(jnp.bfloat16)
            for n in range(4):
                lanes = total[:, n * BLOCK : (n + 1) * BLOCK]
                csend[half, j * 4 + n] = jnp.concatenate([lanes[:112], lanes[112:]], axis=1)
            for n in range(4):
                to_x = (n // 2) * 2 + core
                local = jnp.logical_and(jnp.logical_and(to_x == x, core == n % 2), j == y)

                @pl.when(local)
                def _():
                    pltpu.make_async_copy(
                        csend.at[half, j * 4 + n], crecv.at[half, y * 4 + x], cr.at[half]
                    ).start()

                @pl.when(jnp.logical_not(local))
                def _():
                    rcopy(
                        csend.at[half, j * 4 + n], crecv.at[half, y * 4 + x], cs.at[half],
                        cr.at[half], dev(z, to_x, j, n % 2),
                    ).start()

    def project(half, zsrc):
        @pl.when(core == zsrc // 4)
        def _():
            product(half, lax.rem(zsrc, 4))

    def both(s, carry):
        project(0, lax.rem(z + 8 - s, 8))
        project(0, lax.rem(z + s, 8))
        return carry

    gathered(0)
    project(0, z)
    lax.fori_loop(1, 4, both, 0)
    ring_step(4, 1)
    project(0, lax.rem(z + 4, 8))
    pass_on(1)
    gathered(1)

    def by_distance(i, carry):
        product(1, lax.rem(y + 2 + jnp.where(i == 0, 0, jnp.where(i == 3, 2, 2 * i - 3)), 4))
        return carry

    lax.fori_loop(0, 4, by_distance, 0)

    for part, sem in (
        (lat.at[pl.ds(0, 7), 0], zs.at[0]),
        (lat.at[pl.ds(0, 3), pl.ds(0, 8)], xs.at[0]),
        (lat.at[pl.ds(0, 2)], ys.at[0]),
        (lat.at[pl.ds(0, 4)], ks.at[0]),
    ):
        rcopy(part, part, sem, kr.at[0], other).wait_send()

    @pl.when(jnp.logical_not(at_home))
    def _():
        rcopy(w_hbm, wbuf.at[wj, xl], w0.at[0], wr.at[wj, xl], other).wait_send()

    for q in range(2):
        part = xl if q == 0 else 1 - xl

        @pl.when(core == keeper)
        def _():
            for n in range(2):
                slot = wbuf.at[wj, part]
                rcopy(slot, slot, ws.at[n, wj, part], wr.at[wj, part], other).wait_send()

        for s in range(1, 4):
            for up, part, zsrc, reach in ring_moves(s, q):
                j = lax.rem(zsrc, 4)

                @pl.when(jnp.logical_and(core == zsrc // 4, s < reach))
                def _():
                    slot = wbuf.at[j, part]
                    rcopy(
                        slot, slot, ws.at[0 if up else 1, j, part], wr.at[j, part], other
                    ).wait_send()

    halves = []
    for half in range(2):
        columns = []
        rcopy(crecv.at[half], crecv.at[half], cs.at[half], cr.at[half], other).wait_recv()
        for n in range(4):
            total = None
            for m in range(4):
                term = crecv[half, m * 4 + n].astype(jnp.float32)
                total = term if total is None else total + term
            columns += [total[:, :BLOCK], total[:, BLOCK:]]
        halves.append(jnp.concatenate(columns, axis=0))
    first = jnp.where(low_at == 0, halves[0], halves[1])
    second = jnp.where(low_at == 0, halves[1], halves[0])
    mixed = jnp.concatenate([first, second], axis=1)
    out_ref[...] = jnp.transpose(mixed, (1, 0)).astype(jnp.bfloat16)
    for half in range(2):
        here = shard(half, x, core)
        for n in range(4):
            if n:
                rcopy(here, here, as_.at[half, n], ar.at[half, n], other).wait_send()
            rcopy(here, here, bs.at[half, n], br.at[half, n], other).wait_send()

        @pl.when(core == xl)
        def _():
            most = csend.at[half, pl.ds(0, 15)]
            rcopy(most, most, cs.at[half], cr.at[half], other).wait_send()

        @pl.when(core != xl)
        def _():
            rcopy(csend.at[half], csend.at[half], cs.at[half], cr.at[half], other).wait_send()


def body(queries, latent_rope, key_up, value_up, out_weight, plan):
    vm = pl.BlockSpec(memory_space=pltpu.VMEM)
    sm = pl.BlockSpec(memory_space=pltpu.SMEM)
    anywhere = pl.BlockSpec(memory_space=pl.ANY)
    bf, f32 = jnp.bfloat16, jnp.float32
    dma = pltpu.SemaphoreType.DMA
    return pl.pallas_call(
        kernel,
        out_shape=jax.ShapeDtypeStruct((128, 896), bf),
        in_specs=[sm, anywhere, anywhere, anywhere, anywhere, anywhere],
        out_specs=vm,
        scratch_shapes=[
            pltpu.SMEM((32,), jnp.int32),
            pltpu.VMEM((LATENT + ROPE, 128), bf),
            pltpu.VMEM((8, 16, PIECE, 128), bf),
            pltpu.VMEM((128, 1536), bf),
            pltpu.VMEM((512, 1024), bf),
            pltpu.VMEM((512, 1024), bf),
            pltpu.VMEM((2, ROWS, WIDE), bf),
            pltpu.VMEM((EARLY, ROWS, 256), f32),
            pltpu.VMEM((EARLY + LATE + 1, ROWS, 128), f32),
            pltpu.VMEM((2, ROWS, 128), f32),
            pltpu.VMEM((EARLY + 1, ROWS, 128), f32),
            pltpu.VMEM((EARLY + 1, ROWS, LATENT), f32),
            pltpu.VMEM((4, 2, 224, 1024), bf),
            pltpu.VMEM((2, 2, 2, 2, BLOCK, 1024), bf),
            pltpu.VMEM((2, 16, 112, 128), bf),
            pltpu.VMEM((2, 16, 112, 128), bf),
            dma((4,)), dma((1,)), dma((8,)), dma((1,)), dma((4, 8)), dma((1,)), dma((4, 8)),
            dma((1,)), dma((1,)), dma((1,)), dma((2, 4, 2)), dma((4, 2)),
            dma((2, 4)), dma((2, 4)), dma((2, 4)), dma((2, 4)), dma((2,)), dma((2,)),
        ],
        compiler_params=pltpu.CompilerParams(
            collective_id=0, has_side_effects=True, vmem_limit_bytes=56 * 2**20
        ),
    )(plan.T, latent_rope.T, queries, key_up, value_up, out_weight.T)


def solution(mesh):
    placed = (
        P("ctx", "head"),
        P("ctx", None),
        P(None, "head"),
        P(None, "head"),
        P("head", "ctx"),
        P(),
    )
    return jax.shard_map(
        body, mesh=mesh, in_specs=placed, out_specs=P("ctx", "head"), check_vma=False
    )
```

```python
import jax
import jax.numpy as jnp
from jax import lax
from jax.experimental import pallas as pl
from jax.experimental.pallas import tpu as pltpu
from jax.sharding import PartitionSpec as P

MESH = pl.DeviceIdType.MESH
NOPE = 128
ROPE = 64
VDIM = 128
LATENT = 512
HEAD_LOCAL = 8
BLOCK = 64
ROWS = HEAD_LOCAL * BLOCK
EARLY = 9
LATE = 8
WIDE = 640
PIECE = 144
NEG = -1e30
SCALE2 = 1.4426950408889634 * (NOPE + ROPE) ** -0.5


def nt(a, b):
    return lax.dot_general(a, b, (((1,), (1,)), ((), ())), preferred_element_type=jnp.float32)


def kernel(
    plan_ref, lrt_hbm, q_hbm, ku_hbm, vu_hbm, w_hbm, out_ref,
    place, lrt, lat, qv, kuv, vuv, qs, sbuf, mrun, mfin, lrun, acc, wbuf, att, csend, crecv, fsend, frecv,
    ls, zs, zr, xs, xr, ys, yr, ks, kr, w0, ws, wr, as_, ar, bs, br, cs, cr, fs, fr,
):
    ctx = lax.axis_index("ctx")
    head = lax.axis_index("head")
    core = lax.rem(ctx, 2)
    xh = lax.rem(ctx // 2, 2)
    z = ctx // 4
    xl = head // 4
    y = lax.rem(head, 4)
    x = xh * 2 + xl

    def dev(z_, x_, y_, c_):
        return ((z_ * 2 + x_ // 2) * 2 + c_, lax.rem(x_, 2) * 4 + y_)

    def zdev(d):
        return dev(lax.rem(z + d, 8), x, y, core)

    def xdev(o):
        return dev(z, lax.rem(x + o, 4), y, core)

    def ydev(o):
        return dev(z, x, lax.rem(y + o, 4), core)

    other = dev(z, x, y, 1 - core)

    def rcopy(src, dst, ssem, rsem, target):
        return pltpu.make_async_remote_copy(
            src_ref=src, dst_ref=dst, send_sem=ssem, recv_sem=rsem,
            device_id=target, device_id_type=MESH,
        )

    loads = [
        pltpu.make_async_copy(lrt_hbm, lrt, ls.at[3]),
        pltpu.make_async_copy(q_hbm, qv, ls.at[0]),
        pltpu.make_async_copy(ku_hbm, kuv, ls.at[1]),
        pltpu.make_async_copy(vu_hbm, vuv, ls.at[2]),
    ]
    for cp in loads:
        cp.start()

    barrier = pltpu.get_barrier_semaphore()
    for d in range(1, 8):
        pl.semaphore_signal(barrier, 1, device_id=zdev(d), device_id_type=MESH)
    for oy in range(4):
        for ox in range(4):
            for oc in range(2):
                if oy or ox or oc:
                    pl.semaphore_signal(
                        barrier, 1,
                        device_id=dev(z, lax.rem(x + ox, 4), lax.rem(y + oy, 4), lax.rem(core + oc, 2)),
                        device_id_type=MESH,
                    )
    par = lax.rem(y, 2)

    def piece(src_x, parity, c_):
        return (src_x // 2) * 8 + c_ * 4 + parity * 2 + lax.rem(src_x, 2)

    mine = piece(x, par, core)
    loads[0].wait()
    rows_all = jnp.transpose(lrt[...], (1, 0))
    quarter = par * 2 + xl
    for q in range(4):
        @pl.when(quarter == q)
        def _():
            part = rows_all[q * 32 : (q + 1) * 32]
            for c in range(4):
                lat[z, mine, c * 32 : (c + 1) * 32] = part[:, c * 128 : (c + 1) * 128]
            rope = part[:, LATENT:]
            lat[z, mine, 128:PIECE] = jnp.concatenate([rope[:16], rope[16:]], axis=1)

    def dist(i):
        if isinstance(i, int):
            return 0
        return lax.rem(jnp.where(lax.rem(i, 2) == 1, (i + 1) // 2, 8 - i // 2), 8)

    def source(i):
        return lax.rem(z + 8 - dist(i), 8)

    def spread(o, i, zsrc, idx):
        slot = lat.at[zsrc, idx]
        to = lax.rem(y + 1 + 2 * (i % 2), 4)
        rcopy(slot, slot, ys.at[0], yr.at[o, i], dev(z, x, to, core)).start()
        rcopy(slot, slot, ks.at[0], kr.at[0], other).start()

    pair = x + 1 - 2 * xl
    cross = 3 - x
    origin = (x, pair, cross, lax.rem(x + 2, 4))

    def from_z(i):
        zsrc = source(i)
        slot = lat.at[zsrc, mine]
        d = dist(i)

        if not isinstance(i, int):
            rcopy(slot, slot, zs.at[0], zr.at[d], other).wait_recv()
        rcopy(slot, slot, xs.at[0], xr.at[1, i], dev(z, pair, y, core)).start()
        rcopy(slot, slot, xs.at[0], xr.at[2, i], dev(z, cross, y, core)).start()
        spread(0, i, zsrc, mine)

    def from_x(i, o):
        zsrc = source(i)
        idx = piece(origin[o], par, core)
        slot = lat.at[zsrc, idx]
        rcopy(slot, slot, xs.at[0], xr.at[o, i], other).wait_recv()
        if o == 1:
            rcopy(slot, slot, xs.at[0], xr.at[3, i], dev(z, cross, y, core)).start()
        spread(o, i, zsrc, idx)

    def from_y(i):
        zsrc = source(i)
        for o in range(4):
            idx = piece(origin[o], 1 - par, core)
            slot = lat.at[zsrc, idx]
            rcopy(slot, slot, ys.at[0], yr.at[o, i], other).wait_recv()
            rcopy(slot, slot, ks.at[0], kr.at[0], other).start()

    def stage(m, carry):
        @pl.when(m < 4)
        def _():
            from_z(2 * m + 1)

        @pl.when(m < 3)
        def _():
            from_z(2 * m + 2)

        @pl.when(m < 8)
        def _():
            from_x(m, 1)
            from_x(m, 2)

        @pl.when(jnp.logical_and(m >= 1, m < 9))
        def _():
            from_x(m - 1, 3)

        @pl.when(m >= 3)
        def _():
            from_y(m - 3)

        return carry

    pl.semaphore_wait(barrier, 38)

    for d in (1, 7, 2, 6, 3, 5, 4):
        rcopy(lat.at[z, mine], lat.at[z, mine], zs.at[0], zr.at[d], zdev(d)).start()

    from_z(0)

    wj = lax.rem(z, 4)
    keeper = z // 4
    at_home = jnp.logical_and(core == xl, core == keeper)

    @pl.when(at_home)
    def _():
        pltpu.make_async_copy(w_hbm, wbuf.at[wj, xl], wr.at[wj, xl]).start()

    @pl.when(jnp.logical_not(at_home))
    def _():
        rcopy(
            w_hbm, wbuf.at[wj, xl], w0.at[0], wr.at[wj, xl], dev(z, xh * 2 + core, y, keeper)
        ).start()

    def place_of(b, carry):
        found = jnp.int32(0)
        for c in range(32):
            found = jnp.where(jnp.minimum(plan_ref[0, c], plan_ref[1, c]) == b, c, found)
        place[b] = found
        return carry

    lax.fori_loop(0, 32, place_of, 0)

    for cp in loads[1:]:
        cp.wait()
    for h in range(HEAD_LOCAL):
        lo = h * (NOPE + ROPE)
        qn = qv[:, lo : lo + NOPE]
        qr = qv[:, lo + NOPE : lo + NOPE + ROPE].astype(jnp.float32) * SCALE2
        qr = qr.astype(jnp.bfloat16)
        ql = (nt(qn, kuv[:, h * NOPE : (h + 1) * NOPE]) * SCALE2).astype(jnp.bfloat16)
        qr = jnp.concatenate([qr, qr], axis=1)
        for i in range(2):
            qs[i, h * BLOCK : (h + 1) * BLOCK, 0:LATENT] = ql[i * BLOCK : (i + 1) * BLOCK]
            qs[i, h * BLOCK : (h + 1) * BLOCK, LATENT:WIDE] = qr[i * BLOCK : (i + 1) * BLOCK]

    def ring_send(j, part, up):
        slot = wbuf.at[j, part]
        n = 0 if up else 1
        rcopy(slot, slot, ws.at[n, j, part], wr.at[j, part], zdev(1 if up else 7)).start()

    def ring_wait(j, part):
        slot = wbuf.at[j, part]
        rcopy(slot, slot, w0.at[0], wr.at[j, part], other).wait_recv()

    def ring_moves(s, q):
        part = xl if q == 0 else 1 - xl
        for up in (True, False):
            reach = jnp.where((part == 0) == up, 4, 3)
            yield up, part, lax.rem(z + (8 - s if up else s), 8), reach

    def ring_step(s, q):
        if s == 0:
            part = xl if q == 0 else 1 - xl

            @pl.when(core == keeper)
            def _():
                ring_wait(wj, part)
                ring_send(wj, part, True)
                ring_send(wj, part, False)
            return
        for up, part, zsrc, reach in ring_moves(s, q):
            j = lax.rem(zsrc, 4)

            @pl.when(jnp.logical_and(core == zsrc // 4, s <= reach))
            def _():
                ring_wait(j, part)

            @pl.when(jnp.logical_and(core == zsrc // 4, s < reach))
            def _():
                ring_send(j, part, up)

    ring_step(0, 0)
    lax.fori_loop(0, 2, stage, 0)
    ring_step(0, 1)
    lax.fori_loop(2, 3, stage, 0)
    ring_step(1, 0)
    lax.fori_loop(3, 6, stage, 0)
    ring_step(1, 1)
    lax.fori_loop(6, 9, stage, 0)
    ring_step(2, 0)
    lax.fori_loop(9, 11, stage, 0)

    many = lat.at[pl.ds(0, 4)]
    rcopy(many, many, ks.at[0], kr.at[0], other).wait_recv()
    ring_step(2, 1)

    p0 = plan_ref[0, ctx]
    p1 = plan_ref[1, ctx]
    low = jnp.minimum(p0, p1)
    high = jnp.maximum(p0, p1)
    low_at = jnp.where(p0 < p1, 0, 1)
    beta = lax.div(low, 4)
    ahead = lax.broadcasted_iota(jnp.int32, (BLOCK, 256), 1) - lax.broadcasted_iota(
        jnp.int32, (BLOCK, 256), 0
    )
    left = lax.broadcasted_iota(jnp.int32, (16, 128), 1) < 64
    none = jnp.zeros((16, 128), jnp.bfloat16)

    def chunk_of(t):
        return jnp.where(t <= beta, t, t - beta - 1)

    def pieces_of(t):
        first = chunk_of(t) * 4
        got = []
        for i in range(4):
            c = place[jnp.minimum(first + i, 63 - first - i)]
            s = 2 * c + jnp.where(plan_ref[0, c] == first + i, 0, 1)
            pair = lat[lax.div(s, 8), pl.ds(lax.rem(s, 8) * 2, 2)]
            got += [pair[0], pair[1]]
        return got

    def wide_of(got):
        return jnp.concatenate(
            [
                jnp.concatenate([p[c * 32 : (c + 1) * 32] for p in got], axis=0)
                for c in range(4)
            ],
            axis=1,
        )

    def keys_of(t):
        got = pieces_of(t)
        rope = []
        for p in got:
            r = p[128:PIECE]
            rope += [jnp.where(left, r, none), jnp.where(left, none, r)]
        return jnp.concatenate([wide_of(got), jnp.concatenate(rope, axis=0)], axis=1)

    def values_of(t):
        return wide_of(pieces_of(t))

    def masked(s, first_row, first_key):
        allowed = (ahead <= first_row - first_key)[None]
        return jnp.where(allowed, s.reshape(HEAD_LOCAL, BLOCK, 256), NEG).reshape(ROWS, 256)

    def fold(s):
        return jnp.maximum(s[:, :128], s[:, 128:])

    mrun[0] = jnp.full((ROWS, 128), NEG, jnp.float32)
    lrun[0] = jnp.zeros((ROWS, 128), jnp.float32)
    acc[0] = jnp.zeros((ROWS, LATENT), jnp.float32)

    def score(t, carry):
        is_low = t <= beta
        q = qs[jnp.where(is_low, low_at, 1 - low_at)]
        s = nt(q, keys_of(t))
        s = masked(s, jnp.where(is_low, low, high) * BLOCK, chunk_of(t) * 256)
        sbuf[t] = s
        before = jnp.where(t == beta + 1, NEG, mrun[t])
        mrun[t + 1] = jnp.maximum(before, fold(s))
        return carry

    def row_max(at):
        return jnp.broadcast_to(jnp.max(mrun[at], axis=1, keepdims=True), (ROWS, 128))

    def weights(s, m):
        wa = jnp.exp2(s[:, :128] - m)
        wb = jnp.exp2(s[:, 128:] - m)
        return wa + wb, jnp.concatenate([wa, wb], axis=1).astype(jnp.bfloat16)

    def weigh(t, carry):
        is_low = t <= beta
        keep = jnp.where(t == beta + 1, 0.0, 1.0)
        total, w = weights(sbuf[t], mfin[jnp.where(is_low, 0, 1)])
        lrun[t + 1] = lrun[t] * keep + total
        added = jnp.dot(w, values_of(t), preferred_element_type=jnp.float32)
        acc[t + 1] = acc[t] * keep + added
        return carry

    def normal(at):
        total = jnp.sum(lrun[at], axis=1, keepdims=True)
        return (acc[at] / total).astype(jnp.bfloat16)

    def shard(half, src_x, c_):
        return att.at[half, lax.rem(src_x, 2) * 4 + (src_x // 2) * 2 + c_]

    def finish(half, o):
        for h in range(HEAD_LOCAL):
            up = jnp.dot(
                o[h * BLOCK : (h + 1) * BLOCK],
                vuv[:, h * VDIM : (h + 1) * VDIM],
                preferred_element_type=jnp.float32,
            )
            att[half, xl * 4 + xh * 2 + core, :, h * VDIM : (h + 1) * VDIM] = up.astype(jnp.bfloat16)
        here = shard(half, x, core)
        for n in (2, 1, 3):
            rcopy(here, here, as_.at[half], ar.at[half, n], xdev(n)).start()
        rcopy(here, here, bs.at[half], br.at[half], other).start()

    def pass_on(half):
        for n in (1, 3, 2):
            there = shard(half, lax.rem(x + 4 - n, 4), core)
            rcopy(there, there, as_.at[half], ar.at[half, n], other).wait_recv()
            rcopy(there, there, bs.at[half], br.at[half], other).start()

    def gathered(half):
        four = att.at[half, pl.ds(0, 4)]
        rcopy(four, four, bs.at[half], br.at[half], other).wait_recv()

    lax.fori_loop(0, EARLY, score, 0, unroll=3)
    mfin[0] = row_max(beta + 1)
    mfin[1] = row_max(EARLY)
    lax.fori_loop(0, EARLY, weigh, 0, unroll=3)
    finish(0, normal(beta + 1))
    ring_step(3, 0)

    def late_score(i, carry, last=False):
        t = EARLY + i
        s = nt(qs[1 - low_at], keys_of(t))
        if last:
            s = masked(s, high * BLOCK, chunk_of(t) * 256)
        sbuf[i] = s
        mrun[t + 1] = jnp.maximum(mrun[t], fold(s))
        return carry

    lax.fori_loop(0, LATE - 2, late_score, 0, unroll=3)
    late_score(LATE - 2, 0)
    late_score(LATE - 1, 0, last=True)
    mfin[0] = row_max(EARLY + LATE)
    again = jnp.exp2(mfin[1] - mfin[0])
    lrun[EARLY] = lrun[EARLY] * again
    acc[EARLY] = acc[EARLY] * jnp.concatenate([again] * 4, axis=1)
    ring_step(3, 1)

    def late_weigh(i, carry):
        m = mfin[0]
        total, w = weights(sbuf[2 * i], m)
        total2, w2 = weights(sbuf[2 * i + 1], m)
        lrun[EARLY] = lrun[EARLY] + (total + total2)
        v = jnp.concatenate([values_of(EARLY + 2 * i), values_of(EARLY + 2 * i + 1)], axis=0)
        acc[EARLY] = acc[EARLY] + jnp.dot(
            jnp.concatenate([w, w2], axis=1), v, preferred_element_type=jnp.float32
        )
        return carry

    lax.fori_loop(0, LATE // 2, late_weigh, 0, unroll=2)
    finish(1, normal(EARLY))
    pass_on(0)

    def pack(half, j, total):
        total = total.astype(jnp.bfloat16)
        for n in range(4):
            lanes = total[:, n * BLOCK : (n + 1) * BLOCK]
            csend[half, j * 4 + n] = jnp.concatenate([lanes[:112], lanes[112:]], axis=1)

    def rows_of(half, part):
        return att[half, part * 4 : part * 4 + 4].reshape(256, 1024)

    def project(zsrc):
        @pl.when(core == zsrc // 4)
        def _():
            j = lax.rem(zsrc, 4)
            pack(0, j, nt(wbuf[j, 0], rows_of(0, 0)) + nt(wbuf[j, 1], rows_of(0, 1)))

            @pl.when(j != y)
            def _():
                rcopy(
                    csend.at[0, pl.ds(4 * j, 4)], crecv.at[0, pl.ds(4 * lax.rem(j + 4 - y, 4), 4)],
                    cs.at[0], cr.at[0], dev(z, x, j, core),
                ).start()

    def both(s, carry):
        project(lax.rem(z + 8 - s, 8))
        project(lax.rem(z + s, 8))
        return carry

    gathered(0)
    project(z)
    lax.fori_loop(1, 4, both, 0)
    ring_step(4, 0)
    ring_step(4, 1)
    project(lax.rem(z + 4, 8))
    pass_on(1)
    gathered(1)

    def deliver(i, carry):
        j = lax.rem(y + 2 + jnp.where(i == 0, 0, jnp.where(i == 3, 2, 2 * i - 3)), 4)
        for n in range(4):
            to_x = (n // 2) * 2 + core
            local = jnp.logical_and(jnp.logical_and(to_x == x, core == n % 2), j == y)

            @pl.when(local)
            def _():
                pltpu.make_async_copy(
                    csend.at[1, j * 4 + n], crecv.at[1, y * 4 + x], cr.at[1]
                ).start()

            @pl.when(jnp.logical_not(local))
            def _():
                rcopy(
                    csend.at[1, j * 4 + n], crecv.at[1, y * 4 + x], cs.at[1],
                    cr.at[1], dev(z, to_x, j, n % 2),
                ).start()
        return carry

    total = nt(wbuf[:, 0].reshape(896, 1024), rows_of(1, 0)) + nt(
        wbuf[:, 1].reshape(896, 1024), rows_of(1, 1)
    )
    for j in range(4):
        pack(1, j, total[j * 224 : (j + 1) * 224])
    lax.fori_loop(0, 4, deliver, 0)

    for part, sem in (
        (lat.at[pl.ds(0, 7), 0], zs.at[0]),
        (lat.at[pl.ds(0, 3), pl.ds(0, 8)], xs.at[0]),
        (lat.at[pl.ds(0, 2)], ys.at[0]),
        (lat.at[pl.ds(0, 4)], ks.at[0]),
    ):
        rcopy(part, part, sem, kr.at[0], other).wait_send()

    @pl.when(jnp.logical_not(at_home))
    def _():
        rcopy(w_hbm, wbuf.at[wj, xl], w0.at[0], wr.at[wj, xl], other).wait_send()

    for q in range(2):
        part = xl if q == 0 else 1 - xl

        @pl.when(core == keeper)
        def _():
            for n in range(2):
                slot = wbuf.at[wj, part]
                rcopy(slot, slot, ws.at[n, wj, part], wr.at[wj, part], other).wait_send()

        for s in range(1, 4):
            for up, part, zsrc, reach in ring_moves(s, q):
                j = lax.rem(zsrc, 4)

                @pl.when(jnp.logical_and(core == zsrc // 4, s < reach))
                def _():
                    slot = wbuf.at[j, part]
                    rcopy(
                        slot, slot, ws.at[0 if up else 1, j, part], wr.at[j, part], other
                    ).wait_send()

    three = crecv.at[0, pl.ds(4, 12)]
    rcopy(three, three, cs.at[0], cr.at[0], other).wait_recv()
    total = csend[0, pl.ds(4 * y, 4)].astype(jnp.float32)
    for o in range(1, 4):
        total = total + crecv[0, 4 * o : 4 * o + 4].astype(jnp.float32)
    fsend[...] = total.astype(jnp.bfloat16)
    for n in range(4):
        to_x = (n // 2) * 2 + core
        local = jnp.logical_and(to_x == x, core == n % 2)

        @pl.when(local)
        def _():
            pltpu.make_async_copy(fsend.at[n], frecv.at[x], fr.at[0]).start()

        @pl.when(jnp.logical_not(local))
        def _():
            rcopy(
                fsend.at[n], frecv.at[x], fs.at[0], fr.at[0], dev(z, to_x, y, n % 2)
            ).start()

    rcopy(frecv, frecv, fs.at[0], fr.at[0], other).wait_recv()
    rcopy(crecv.at[1], crecv.at[1], cs.at[1], cr.at[1], other).wait_recv()
    columns = [[], []]
    for n in range(4):
        total = crecv[1, n].astype(jnp.float32)
        for m in range(1, 4):
            total = total + crecv[1, m * 4 + n].astype(jnp.float32)
        for half, part in ((0, frecv[n].astype(jnp.float32)), (1, total)):
            columns[half] += [part[:, :BLOCK], part[:, BLOCK:]]
    halves = [jnp.concatenate(c, axis=0) for c in columns]
    first = jnp.where(low_at == 0, halves[0], halves[1])
    second = jnp.where(low_at == 0, halves[1], halves[0])
    mixed = jnp.concatenate([first, second], axis=1)
    out_ref[...] = jnp.transpose(mixed, (1, 0)).astype(jnp.bfloat16)

    for half in range(2):
        for count, sem in ((3, as_.at[half]), (4, bs.at[half])):
            some = att.at[half, pl.ds(0, count)]
            rcopy(some, some, sem, br.at[half], other).wait_send()
    rcopy(three, three, cs.at[0], cr.at[0], other).wait_send()

    @pl.when(core == xl)
    def _():
        home = fsend.at[pl.ds(0, 3)]
        rcopy(home, home, fs.at[0], fr.at[0], other).wait_send()
        sent = csend.at[1, pl.ds(0, 15)]
        rcopy(sent, sent, cs.at[1], cr.at[1], other).wait_send()

    @pl.when(core != xl)
    def _():
        rcopy(fsend, fsend, fs.at[0], fr.at[0], other).wait_send()
        rcopy(csend.at[1], csend.at[1], cs.at[1], cr.at[1], other).wait_send()


def body(queries, latent_rope, key_up, value_up, out_weight, plan):
    vm = pl.BlockSpec(memory_space=pltpu.VMEM)
    sm = pl.BlockSpec(memory_space=pltpu.SMEM)
    anywhere = pl.BlockSpec(memory_space=pl.ANY)
    bf, f32 = jnp.bfloat16, jnp.float32
    dma = pltpu.SemaphoreType.DMA
    return pl.pallas_call(
        kernel,
        out_shape=jax.ShapeDtypeStruct((128, 896), bf),
        in_specs=[sm, anywhere, anywhere, anywhere, anywhere, anywhere],
        out_specs=vm,
        scratch_shapes=[
            pltpu.SMEM((32,), jnp.int32),
            pltpu.VMEM((LATENT + ROPE, 128), bf),
            pltpu.VMEM((8, 16, PIECE, 128), bf),
            pltpu.VMEM((128, 1536), bf),
            pltpu.VMEM((512, 1024), bf),
            pltpu.VMEM((512, 1024), bf),
            pltpu.VMEM((2, ROWS, WIDE), bf),
            pltpu.VMEM((EARLY, ROWS, 256), f32),
            pltpu.VMEM((EARLY + LATE + 1, ROWS, 128), f32),
            pltpu.VMEM((2, ROWS, 128), f32),
            pltpu.VMEM((EARLY + 1, ROWS, 128), f32),
            pltpu.VMEM((EARLY + 1, ROWS, LATENT), f32),
            pltpu.VMEM((4, 2, 224, 1024), bf),
            pltpu.VMEM((2, 8, BLOCK, 1024), bf),
            pltpu.VMEM((2, 16, 112, 128), bf),
            pltpu.VMEM((2, 16, 112, 128), bf),
            pltpu.VMEM((4, 112, 128), bf),
            pltpu.VMEM((4, 112, 128), bf),
            dma((4,)), dma((1,)), dma((8,)), dma((1,)), dma((4, 8)), dma((1,)), dma((4, 8)),
            dma((1,)), dma((1,)), dma((1,)), dma((2, 4, 2)), dma((4, 2)),
            dma((2,)), dma((2, 4)), dma((2,)), dma((2,)), dma((2,)), dma((2,)), dma((1,)), dma((1,)),
        ],
        compiler_params=pltpu.CompilerParams(
            collective_id=0, has_side_effects=True, vmem_limit_bytes=56 * 2**20
        ),
    )(plan.T, latent_rope.T, queries, key_up, value_up, out_weight.T)


def solution(mesh):
    placed = (
        P("ctx", "head"),
        P("ctx", None),
        P(None, "head"),
        P(None, "head"),
        P("head", "ctx"),
        P(),
    )
    return jax.shard_map(
        body, mesh=mesh, in_specs=placed, out_specs=P("ctx", "head"), check_vma=False
    )
```

```python
import jax
import jax.numpy as jnp
from jax import lax
from jax.experimental import pallas as pl
from jax.experimental.pallas import tpu as pltpu
from jax.sharding import PartitionSpec as P

MESH = pl.DeviceIdType.MESH
NOPE = 128
ROPE = 64
VDIM = 128
LATENT = 512
HEAD_LOCAL = 8
BLOCK = 64
ROWS = HEAD_LOCAL * BLOCK
EARLY = 9
LATE = 8
WIDE = 640
PIECE = 144
NEG = -1e30
SCALE2 = 1.4426950408889634 * (NOPE + ROPE) ** -0.5


def nt(a, b):
    return lax.dot_general(a, b, (((1,), (1,)), ((), ())), preferred_element_type=jnp.float32)


def kernel(
    plan_hbm, lrt_hbm, q_hbm, ku_hbm, vu_hbm, w_hbm, out_ref,
    plan_ref, place, lrt, lat, qv, kuv, vuv, qs, sbuf, mrun, mfin, lrun, acc, wbuf, att, csend, crecv, fsend, frecv,
    ls, zs, zr, xs, xr, ys, yr, ks, kr, w0, ws, wr, as_, ar, bs, br, cs, cr, fs, fr,
):
    ctx = lax.axis_index("ctx")
    head = lax.axis_index("head")
    core = lax.rem(ctx, 2)
    xh = lax.rem(ctx // 2, 2)
    z = ctx // 4
    xl = head // 4
    y = lax.rem(head, 4)
    x = xh * 2 + xl

    def dev(z_, x_, y_, c_):
        return ((z_ * 2 + x_ // 2) * 2 + c_, lax.rem(x_, 2) * 4 + y_)

    def zdev(d):
        return dev(lax.rem(z + d, 8), x, y, core)

    def xdev(o):
        return dev(z, lax.rem(x + o, 4), y, core)

    def ydev(o):
        return dev(z, x, lax.rem(y + o, 4), core)

    other = dev(z, x, y, 1 - core)

    def rcopy(src, dst, ssem, rsem, target):
        return pltpu.make_async_remote_copy(
            src_ref=src, dst_ref=dst, send_sem=ssem, recv_sem=rsem,
            device_id=target, device_id_type=MESH,
        )

    loads = [
        pltpu.make_async_copy(lrt_hbm, lrt, ls.at[3]),
        pltpu.make_async_copy(q_hbm, qv, ls.at[0]),
        pltpu.make_async_copy(ku_hbm, kuv, ls.at[1]),
        pltpu.make_async_copy(vu_hbm, vuv, ls.at[2]),
        pltpu.make_async_copy(plan_hbm, plan_ref, ls.at[4]),
    ]
    for cp in loads:
        cp.start()

    barrier = pltpu.get_barrier_semaphore()
    for d in range(1, 8):
        pl.semaphore_signal(barrier, 1, device_id=zdev(d), device_id_type=MESH)
    for oy in range(4):
        for ox in range(4):
            for oc in range(2):
                if oy or ox or oc:
                    pl.semaphore_signal(
                        barrier, 1,
                        device_id=dev(z, lax.rem(x + ox, 4), lax.rem(y + oy, 4), lax.rem(core + oc, 2)),
                        device_id_type=MESH,
                    )
    par = lax.rem(y, 2)

    def piece(src_x, parity, c_):
        return (src_x // 2) * 8 + c_ * 4 + parity * 2 + lax.rem(src_x, 2)

    mine = piece(x, par, core)
    loads[0].wait()
    rows_all = jnp.transpose(lrt[...], (1, 0))
    quarter = par * 2 + xl
    for q in range(4):
        @pl.when(quarter == q)
        def _():
            part = rows_all[q * 32 : (q + 1) * 32]
            for c in range(4):
                lat[z, mine, c * 32 : (c + 1) * 32] = part[:, c * 128 : (c + 1) * 128]
            rope = part[:, LATENT:]
            lat[z, mine, 128:PIECE] = jnp.concatenate([rope[:16], rope[16:]], axis=1)

    def dist(i):
        if isinstance(i, int):
            return 0
        return lax.rem(jnp.where(lax.rem(i, 2) == 1, (i + 1) // 2, 8 - i // 2), 8)

    def source(i):
        return lax.rem(z + 8 - dist(i), 8)

    def spread(o, i, zsrc, idx):
        slot = lat.at[zsrc, idx]
        to = lax.rem(y + 1 + 2 * (i % 2), 4)
        rcopy(slot, slot, ys.at[0], yr.at[o, i], dev(z, x, to, core)).start()
        rcopy(slot, slot, ks.at[0], kr.at[0], other).start()

    pair = x + 1 - 2 * xl
    cross = 3 - x
    origin = (x, pair, cross, lax.rem(x + 2, 4))

    def from_z(i):
        zsrc = source(i)
        slot = lat.at[zsrc, mine]
        d = dist(i)

        if not isinstance(i, int):
            rcopy(slot, slot, zs.at[0], zr.at[d], other).wait_recv()
        rcopy(slot, slot, xs.at[0], xr.at[1, i], dev(z, pair, y, core)).start()
        rcopy(slot, slot, xs.at[0], xr.at[2, i], dev(z, cross, y, core)).start()
        spread(0, i, zsrc, mine)

    def from_x(i, o):
        zsrc = source(i)
        idx = piece(origin[o], par, core)
        slot = lat.at[zsrc, idx]
        rcopy(slot, slot, xs.at[0], xr.at[o, i], other).wait_recv()
        if o == 1:
            rcopy(slot, slot, xs.at[0], xr.at[3, i], dev(z, cross, y, core)).start()
        spread(o, i, zsrc, idx)

    def from_y(i):
        zsrc = source(i)
        for o in range(4):
            idx = piece(origin[o], 1 - par, core)
            slot = lat.at[zsrc, idx]
            rcopy(slot, slot, ys.at[0], yr.at[o, i], other).wait_recv()
            rcopy(slot, slot, ks.at[0], kr.at[0], other).start()

    def stage(m, carry):
        @pl.when(m < 4)
        def _():
            from_z(2 * m + 1)

        @pl.when(m < 3)
        def _():
            from_z(2 * m + 2)

        @pl.when(m < 8)
        def _():
            from_x(m, 1)
            from_x(m, 2)

        @pl.when(jnp.logical_and(m >= 1, m < 9))
        def _():
            from_x(m - 1, 3)

        @pl.when(m >= 3)
        def _():
            from_y(m - 3)

        return carry

    pl.semaphore_wait(barrier, 38)

    for d in (1, 7, 2, 6, 3, 5, 4):
        rcopy(lat.at[z, mine], lat.at[z, mine], zs.at[0], zr.at[d], zdev(d)).start()

    from_z(0)

    wj = lax.rem(z, 4)
    keeper = z // 4
    at_home = jnp.logical_and(core == xl, core == keeper)

    @pl.when(at_home)
    def _():
        pltpu.make_async_copy(w_hbm, wbuf.at[wj, xl], wr.at[wj, xl]).start()

    @pl.when(jnp.logical_not(at_home))
    def _():
        rcopy(
            w_hbm, wbuf.at[wj, xl], w0.at[0], wr.at[wj, xl], dev(z, xh * 2 + core, y, keeper)
        ).start()

    def place_of(b, carry):
        found = jnp.int32(0)
        for c in range(32):
            found = jnp.where(jnp.minimum(plan_ref[0, c], plan_ref[1, c]) == b, c, found)
        place[b] = found
        return carry

    loads[4].wait()
    lax.fori_loop(0, 32, place_of, 0)

    for cp in loads[1:4]:
        cp.wait()
    for h in range(HEAD_LOCAL):
        lo = h * (NOPE + ROPE)
        qn = qv[:, lo : lo + NOPE]
        qr = qv[:, lo + NOPE : lo + NOPE + ROPE].astype(jnp.float32) * SCALE2
        qr = qr.astype(jnp.bfloat16)
        ql = (nt(qn, kuv[:, h * NOPE : (h + 1) * NOPE]) * SCALE2).astype(jnp.bfloat16)
        qr = jnp.concatenate([qr, qr], axis=1)
        for i in range(2):
            qs[i, h * BLOCK : (h + 1) * BLOCK, 0:LATENT] = ql[i * BLOCK : (i + 1) * BLOCK]
            qs[i, h * BLOCK : (h + 1) * BLOCK, LATENT:WIDE] = qr[i * BLOCK : (i + 1) * BLOCK]

    def ring_send(j, part, up):
        slot = wbuf.at[j, part]
        n = 0 if up else 1
        rcopy(slot, slot, ws.at[n, j, part], wr.at[j, part], zdev(1 if up else 7)).start()

    def ring_wait(j, part):
        slot = wbuf.at[j, part]
        rcopy(slot, slot, w0.at[0], wr.at[j, part], other).wait_recv()

    def ring_moves(s, q):
        part = xl if q == 0 else 1 - xl
        for up in (True, False):
            reach = jnp.where((part == 0) == up, 4, 3)
            yield up, part, lax.rem(z + (8 - s if up else s), 8), reach

    def ring_step(s, q):
        if s == 0:
            part = xl if q == 0 else 1 - xl

            @pl.when(core == keeper)
            def _():
                ring_wait(wj, part)
                ring_send(wj, part, True)
                ring_send(wj, part, False)
            return
        for up, part, zsrc, reach in ring_moves(s, q):
            j = lax.rem(zsrc, 4)

            @pl.when(jnp.logical_and(core == zsrc // 4, s <= reach))
            def _():
                ring_wait(j, part)

            @pl.when(jnp.logical_and(core == zsrc // 4, s < reach))
            def _():
                ring_send(j, part, up)

    ring_step(0, 0)
    lax.fori_loop(0, 2, stage, 0)
    ring_step(0, 1)
    lax.fori_loop(2, 3, stage, 0)
    ring_step(1, 0)
    lax.fori_loop(3, 6, stage, 0)
    ring_step(1, 1)
    lax.fori_loop(6, 9, stage, 0)
    ring_step(2, 0)
    lax.fori_loop(9, 11, stage, 0)

    many = lat.at[pl.ds(0, 4)]
    rcopy(many, many, ks.at[0], kr.at[0], other).wait_recv()
    ring_step(2, 1)

    p0 = plan_ref[0, ctx]
    p1 = plan_ref[1, ctx]
    low = jnp.minimum(p0, p1)
    high = jnp.maximum(p0, p1)
    low_at = jnp.where(p0 < p1, 0, 1)
    beta = lax.div(low, 4)
    ahead = lax.broadcasted_iota(jnp.int32, (BLOCK, 256), 1) - lax.broadcasted_iota(
        jnp.int32, (BLOCK, 256), 0
    )
    left = lax.broadcasted_iota(jnp.int32, (16, 128), 1) < 64
    none = jnp.zeros((16, 128), jnp.bfloat16)

    def chunk_of(t):
        return jnp.where(t <= beta, t, t - beta - 1)

    def pieces_of(t):
        first = chunk_of(t) * 4
        got = []
        for i in range(4):
            c = place[jnp.minimum(first + i, 63 - first - i)]
            s = 2 * c + jnp.where(plan_ref[0, c] == first + i, 0, 1)
            pair = lat[lax.div(s, 8), pl.ds(lax.rem(s, 8) * 2, 2)]
            got += [pair[0], pair[1]]
        return got

    def wide_of(got):
        return jnp.concatenate(
            [
                jnp.concatenate([p[c * 32 : (c + 1) * 32] for p in got], axis=0)
                for c in range(4)
            ],
            axis=1,
        )

    def keys_of(t):
        got = pieces_of(t)
        rope = []
        for p in got:
            r = p[128:PIECE]
            rope += [jnp.where(left, r, none), jnp.where(left, none, r)]
        return jnp.concatenate([wide_of(got), jnp.concatenate(rope, axis=0)], axis=1)

    def values_of(t):
        return wide_of(pieces_of(t))

    def masked(s, first_row, first_key):
        allowed = (ahead <= first_row - first_key)[None]
        return jnp.where(allowed, s.reshape(HEAD_LOCAL, BLOCK, 256), NEG).reshape(ROWS, 256)

    def fold(s):
        return jnp.maximum(s[:, :128], s[:, 128:])

    mrun[0] = jnp.full((ROWS, 128), NEG, jnp.float32)
    lrun[0] = jnp.zeros((ROWS, 128), jnp.float32)
    acc[0] = jnp.zeros((ROWS, LATENT), jnp.float32)

    def score(t, carry):
        is_low = t <= beta
        q = qs[jnp.where(is_low, low_at, 1 - low_at)]
        s = nt(q, keys_of(t))
        s = masked(s, jnp.where(is_low, low, high) * BLOCK, chunk_of(t) * 256)
        sbuf[t] = s
        before = jnp.where(t == beta + 1, NEG, mrun[t])
        mrun[t + 1] = jnp.maximum(before, fold(s))
        return carry

    def row_max(at):
        return jnp.broadcast_to(jnp.max(mrun[at], axis=1, keepdims=True), (ROWS, 128))

    def weights(s, m):
        wa = jnp.exp2(s[:, :128] - m)
        wb = jnp.exp2(s[:, 128:] - m)
        return wa + wb, jnp.concatenate([wa, wb], axis=1).astype(jnp.bfloat16)

    def weigh(t, carry):
        is_low = t <= beta
        keep = jnp.where(t == beta + 1, 0.0, 1.0)
        total, w = weights(sbuf[t], mfin[jnp.where(is_low, 0, 1)])
        lrun[t + 1] = lrun[t] * keep + total
        added = jnp.dot(w, values_of(t), preferred_element_type=jnp.float32)
        acc[t + 1] = acc[t] * keep + added
        return carry

    def normal(at):
        total = jnp.sum(lrun[at], axis=1, keepdims=True)
        return (acc[at] / total).astype(jnp.bfloat16)

    def shard(half, src_x, c_):
        return att.at[half, lax.rem(src_x, 2) * 4 + (src_x // 2) * 2 + c_]

    def finish(half, o):
        for h in range(HEAD_LOCAL):
            up = jnp.dot(
                o[h * BLOCK : (h + 1) * BLOCK],
                vuv[:, h * VDIM : (h + 1) * VDIM],
                preferred_element_type=jnp.float32,
            )
            att[half, xl * 4 + xh * 2 + core, :, h * VDIM : (h + 1) * VDIM] = up.astype(jnp.bfloat16)
        here = shard(half, x, core)
        for n in (2, 1, 3):
            rcopy(here, here, as_.at[half], ar.at[half, n], xdev(n)).start()
        rcopy(here, here, bs.at[half], br.at[half], other).start()

    def pass_on(half):
        for n in (1, 3, 2):
            there = shard(half, lax.rem(x + 4 - n, 4), core)
            rcopy(there, there, as_.at[half], ar.at[half, n], other).wait_recv()
            rcopy(there, there, bs.at[half], br.at[half], other).start()

    def gathered(half):
        four = att.at[half, pl.ds(0, 4)]
        rcopy(four, four, bs.at[half], br.at[half], other).wait_recv()

    lax.fori_loop(0, EARLY, score, 0, unroll=3)
    mfin[0] = row_max(beta + 1)
    mfin[1] = row_max(EARLY)
    lax.fori_loop(0, EARLY, weigh, 0, unroll=3)
    finish(0, normal(beta + 1))
    ring_step(3, 0)

    def late_score(i, carry, last=False):
        t = EARLY + i
        s = nt(qs[1 - low_at], keys_of(t))
        if last:
            s = masked(s, high * BLOCK, chunk_of(t) * 256)
        sbuf[i] = s
        mrun[t + 1] = jnp.maximum(mrun[t], fold(s))
        return carry

    lax.fori_loop(0, LATE - 2, late_score, 0, unroll=3)
    late_score(LATE - 2, 0)
    late_score(LATE - 1, 0, last=True)
    mfin[0] = row_max(EARLY + LATE)
    again = jnp.exp2(mfin[1] - mfin[0])
    lrun[EARLY] = lrun[EARLY] * again
    acc[EARLY] = acc[EARLY] * jnp.concatenate([again] * 4, axis=1)

    def late_weigh(i, carry):
        m = mfin[0]
        total, w = weights(sbuf[2 * i], m)
        total2, w2 = weights(sbuf[2 * i + 1], m)
        lrun[EARLY] = lrun[EARLY] + (total + total2)
        v = jnp.concatenate([values_of(EARLY + 2 * i), values_of(EARLY + 2 * i + 1)], axis=0)
        acc[EARLY] = acc[EARLY] + jnp.dot(
            jnp.concatenate([w, w2], axis=1), v, preferred_element_type=jnp.float32
        )
        return carry

    lax.fori_loop(0, LATE // 2, late_weigh, 0, unroll=2)
    ring_step(3, 1)
    finish(1, normal(EARLY))
    pass_on(0)

    def pack(half, j, total):
        total = total.astype(jnp.bfloat16)
        for n in range(4):
            lanes = total[:, n * BLOCK : (n + 1) * BLOCK]
            csend[half, j * 4 + n] = jnp.concatenate([lanes[:112], lanes[112:]], axis=1)

    def rows_of(half, part):
        return att[half, part * 4 : part * 4 + 4].reshape(256, 1024)

    def project(zsrc):
        @pl.when(core == zsrc // 4)
        def _():
            j = lax.rem(zsrc, 4)
            pack(0, j, nt(wbuf[j, 0], rows_of(0, 0)) + nt(wbuf[j, 1], rows_of(0, 1)))

            @pl.when(j != y)
            def _():
                rcopy(
                    csend.at[0, pl.ds(4 * j, 4)], crecv.at[0, pl.ds(4 * lax.rem(j + 4 - y, 4), 4)],
                    cs.at[0], cr.at[0], dev(z, x, j, core),
                ).start()

    def both(s, carry):
        project(lax.rem(z + 8 - s, 8))
        project(lax.rem(z + s, 8))
        return carry

    gathered(0)
    project(z)
    lax.fori_loop(1, 4, both, 0)
    ring_step(4, 0)
    ring_step(4, 1)
    project(lax.rem(z + 4, 8))
    pass_on(1)
    gathered(1)

    def deliver(i, carry):
        j = lax.rem(y + 2 + jnp.where(i == 0, 0, jnp.where(i == 3, 2, 2 * i - 3)), 4)
        for n in range(4):
            to_x = (n // 2) * 2 + core
            local = jnp.logical_and(jnp.logical_and(to_x == x, core == n % 2), j == y)

            @pl.when(local)
            def _():
                pltpu.make_async_copy(
                    csend.at[1, j * 4 + n], crecv.at[1, y * 4 + x], cr.at[1]
                ).start()

            @pl.when(jnp.logical_not(local))
            def _():
                rcopy(
                    csend.at[1, j * 4 + n], crecv.at[1, y * 4 + x], cs.at[1],
                    cr.at[1], dev(z, to_x, j, n % 2),
                ).start()
        return carry

    total = nt(wbuf[:, 0].reshape(896, 1024), rows_of(1, 0)) + nt(
        wbuf[:, 1].reshape(896, 1024), rows_of(1, 1)
    )
    for j in range(4):
        pack(1, j, total[j * 224 : (j + 1) * 224])
    lax.fori_loop(0, 4, deliver, 0)

    for part, sem in (
        (lat.at[pl.ds(0, 7), 0], zs.at[0]),
        (lat.at[pl.ds(0, 3), pl.ds(0, 8)], xs.at[0]),
        (lat.at[pl.ds(0, 2)], ys.at[0]),
        (lat.at[pl.ds(0, 4)], ks.at[0]),
    ):
        rcopy(part, part, sem, kr.at[0], other).wait_send()

    @pl.when(jnp.logical_not(at_home))
    def _():
        rcopy(w_hbm, wbuf.at[wj, xl], w0.at[0], wr.at[wj, xl], other).wait_send()

    for q in range(2):
        part = xl if q == 0 else 1 - xl

        @pl.when(core == keeper)
        def _():
            for n in range(2):
                slot = wbuf.at[wj, part]
                rcopy(slot, slot, ws.at[n, wj, part], wr.at[wj, part], other).wait_send()

        for s in range(1, 4):
            for up, part, zsrc, reach in ring_moves(s, q):
                j = lax.rem(zsrc, 4)

                @pl.when(jnp.logical_and(core == zsrc // 4, s < reach))
                def _():
                    slot = wbuf.at[j, part]
                    rcopy(
                        slot, slot, ws.at[0 if up else 1, j, part], wr.at[j, part], other
                    ).wait_send()

    three = crecv.at[0, pl.ds(4, 12)]
    rcopy(three, three, cs.at[0], cr.at[0], other).wait_recv()
    total = csend[0, pl.ds(4 * y, 4)].astype(jnp.float32)
    for o in range(1, 4):
        total = total + crecv[0, 4 * o : 4 * o + 4].astype(jnp.float32)
    fsend[...] = total.astype(jnp.bfloat16)
    for n in range(4):
        to_x = (n // 2) * 2 + core
        local = jnp.logical_and(to_x == x, core == n % 2)

        @pl.when(local)
        def _():
            pltpu.make_async_copy(fsend.at[n], frecv.at[x], fr.at[0]).start()

        @pl.when(jnp.logical_not(local))
        def _():
            rcopy(
                fsend.at[n], frecv.at[x], fs.at[0], fr.at[0], dev(z, to_x, y, n % 2)
            ).start()

    rcopy(frecv, frecv, fs.at[0], fr.at[0], other).wait_recv()
    rcopy(crecv.at[1], crecv.at[1], cs.at[1], cr.at[1], other).wait_recv()
    columns = [[], []]
    for n in range(4):
        total = crecv[1, n].astype(jnp.float32)
        for m in range(1, 4):
            total = total + crecv[1, m * 4 + n].astype(jnp.float32)
        for half, part in ((0, frecv[n].astype(jnp.float32)), (1, total)):
            columns[half] += [part[:, :BLOCK], part[:, BLOCK:]]
    halves = [jnp.concatenate(c, axis=0) for c in columns]
    first = jnp.where(low_at == 0, halves[0], halves[1])
    second = jnp.where(low_at == 0, halves[1], halves[0])
    mixed = jnp.concatenate([first, second], axis=1)
    out_ref[...] = jnp.transpose(mixed, (1, 0)).astype(jnp.bfloat16)

    for half in range(2):
        for count, sem in ((3, as_.at[half]), (4, bs.at[half])):
            some = att.at[half, pl.ds(0, count)]
            rcopy(some, some, sem, br.at[half], other).wait_send()
    rcopy(three, three, cs.at[0], cr.at[0], other).wait_send()

    @pl.when(core == xl)
    def _():
        home = fsend.at[pl.ds(0, 3)]
        rcopy(home, home, fs.at[0], fr.at[0], other).wait_send()
        sent = csend.at[1, pl.ds(0, 15)]
        rcopy(sent, sent, cs.at[1], cr.at[1], other).wait_send()

    @pl.when(core != xl)
    def _():
        rcopy(fsend, fsend, fs.at[0], fr.at[0], other).wait_send()
        rcopy(csend.at[1], csend.at[1], cs.at[1], cr.at[1], other).wait_send()


def body(queries, latent_rope, key_up, value_up, out_weight, plan):
    vm = pl.BlockSpec(memory_space=pltpu.VMEM)
    anywhere = pl.BlockSpec(memory_space=pl.ANY)
    bf, f32 = jnp.bfloat16, jnp.float32
    dma = pltpu.SemaphoreType.DMA
    return pl.pallas_call(
        kernel,
        out_shape=jax.ShapeDtypeStruct((128, 896), bf),
        in_specs=[anywhere, anywhere, anywhere, anywhere, anywhere, anywhere],
        out_specs=vm,
        scratch_shapes=[
            pltpu.SMEM((2, 32), jnp.int32),
            pltpu.SMEM((32,), jnp.int32),
            pltpu.VMEM((LATENT + ROPE, 128), bf),
            pltpu.VMEM((8, 16, PIECE, 128), bf),
            pltpu.VMEM((128, 1536), bf),
            pltpu.VMEM((512, 1024), bf),
            pltpu.VMEM((512, 1024), bf),
            pltpu.VMEM((2, ROWS, WIDE), bf),
            pltpu.VMEM((EARLY, ROWS, 256), f32),
            pltpu.VMEM((EARLY + LATE + 1, ROWS, 128), f32),
            pltpu.VMEM((2, ROWS, 128), f32),
            pltpu.VMEM((EARLY + 1, ROWS, 128), f32),
            pltpu.VMEM((EARLY + 1, ROWS, LATENT), f32),
            pltpu.VMEM((4, 2, 224, 1024), bf),
            pltpu.VMEM((2, 8, BLOCK, 1024), bf),
            pltpu.VMEM((2, 16, 112, 128), bf),
            pltpu.VMEM((2, 16, 112, 128), bf),
            pltpu.VMEM((4, 112, 128), bf),
            pltpu.VMEM((4, 112, 128), bf),
            dma((5,)), dma((1,)), dma((8,)), dma((1,)), dma((4, 8)), dma((1,)), dma((4, 8)),
            dma((1,)), dma((1,)), dma((1,)), dma((2, 4, 2)), dma((4, 2)),
            dma((2,)), dma((2, 4)), dma((2,)), dma((2,)), dma((2,)), dma((2,)), dma((1,)), dma((1,)),
        ],
        compiler_params=pltpu.CompilerParams(
            collective_id=0, has_side_effects=True, vmem_limit_bytes=56 * 2**20
        ),
    )(plan.T, latent_rope.T, queries, key_up, value_up, out_weight.T)


def solution(mesh):
    placed = (
        P("ctx", "head"),
        P("ctx", None),
        P(None, "head"),
        P(None, "head"),
        P("head", "ctx"),
        P(),
    )
    return jax.shard_map(
        body, mesh=mesh, in_specs=placed, out_specs=P("ctx", "head"), check_vma=False
    )
```

```python
import jax
import jax.numpy as jnp
from jax import lax
from jax.experimental import pallas as pl
from jax.experimental.pallas import tpu as pltpu
from jax.sharding import PartitionSpec as P

MESH = pl.DeviceIdType.MESH
NOPE = 128
ROPE = 64
VDIM = 128
LATENT = 512
HEAD_LOCAL = 8
BLOCK = 64
ROWS = HEAD_LOCAL * BLOCK
EARLY = 9
LATE = 8
WIDE = 640
PIECE = 144
NEG = -1e30
SCALE2 = 1.4426950408889634 * (NOPE + ROPE) ** -0.5


def nt(a, b):
    return lax.dot_general(a, b, (((1,), (1,)), ((), ())), preferred_element_type=jnp.float32)


def kernel(
    plan_hbm, lrt_hbm, q_hbm, ku_hbm, vu_hbm, w_hbm, out_ref,
    plan_ref, place, lrt, lat, qv, kuv, vuv, qs, sbuf, mrun, mfin, lrun, acc, wbuf, att, csend, crecv, fsend, frecv,
    ls, zs, zr, xs, xr, ys, yr, ks, kr, w0, ws, wr, as_, ar, bs, br, cs, cr, fs, fr,
):
    ctx = lax.axis_index("ctx")
    head = lax.axis_index("head")
    core = lax.rem(ctx, 2)
    xh = lax.rem(ctx // 2, 2)
    z = ctx // 4
    xl = head // 4
    y = lax.rem(head, 4)
    x = xh * 2 + xl

    def dev(z_, x_, y_, c_):
        return ((z_ * 2 + x_ // 2) * 2 + c_, lax.rem(x_, 2) * 4 + y_)

    def zdev(d):
        return dev(lax.rem(z + d, 8), x, y, core)

    def xdev(o):
        return dev(z, lax.rem(x + o, 4), y, core)

    def ydev(o):
        return dev(z, x, lax.rem(y + o, 4), core)

    other = dev(z, x, y, 1 - core)

    def rcopy(src, dst, ssem, rsem, target):
        return pltpu.make_async_remote_copy(
            src_ref=src, dst_ref=dst, send_sem=ssem, recv_sem=rsem,
            device_id=target, device_id_type=MESH,
        )

    loads = [
        pltpu.make_async_copy(lrt_hbm, lrt, ls.at[3]),
        pltpu.make_async_copy(q_hbm, qv, ls.at[0]),
        pltpu.make_async_copy(ku_hbm, kuv, ls.at[1]),
        pltpu.make_async_copy(vu_hbm, vuv, ls.at[2]),
        pltpu.make_async_copy(plan_hbm, plan_ref, ls.at[4]),
    ]
    for cp in loads:
        cp.start()

    barrier = pltpu.get_barrier_semaphore()
    for d in range(1, 8):
        pl.semaphore_signal(barrier, 1, device_id=zdev(d), device_id_type=MESH)
    for oy in range(4):
        for ox in range(4):
            for oc in range(2):
                if oy or ox or oc:
                    pl.semaphore_signal(
                        barrier, 1,
                        device_id=dev(z, lax.rem(x + ox, 4), lax.rem(y + oy, 4), lax.rem(core + oc, 2)),
                        device_id_type=MESH,
                    )
    par = lax.rem(y, 2)

    def piece(src_x, parity, c_):
        return (src_x // 2) * 8 + c_ * 4 + parity * 2 + lax.rem(src_x, 2)

    mine = piece(x, par, core)
    loads[0].wait()
    rows_all = jnp.transpose(lrt[...], (1, 0))
    quarter = par * 2 + xl
    for q in range(4):
        @pl.when(quarter == q)
        def _():
            part = rows_all[q * 32 : (q + 1) * 32]
            for c in range(4):
                lat[z, mine, c * 32 : (c + 1) * 32] = part[:, c * 128 : (c + 1) * 128]
            rope = part[:, LATENT:]
            lat[z, mine, 128:PIECE] = jnp.concatenate([rope[:16], rope[16:]], axis=1)

    def dist(i):
        if isinstance(i, int):
            return 0
        return lax.rem(jnp.where(lax.rem(i, 2) == 1, (i + 1) // 2, 8 - i // 2), 8)

    def source(i):
        return lax.rem(z + 8 - dist(i), 8)

    def spread(o, i, zsrc, idx):
        slot = lat.at[zsrc, idx]
        to = lax.rem(y + 1 + 2 * (i % 2), 4)
        rcopy(slot, slot, ys.at[0], yr.at[o, i], dev(z, x, to, core)).start()
        rcopy(slot, slot, ks.at[0], kr.at[0], other).start()

    pair = x + 1 - 2 * xl
    cross = 3 - x
    origin = (x, pair, cross, lax.rem(x + 2, 4))

    def from_z(i):
        zsrc = source(i)
        slot = lat.at[zsrc, mine]
        d = dist(i)

        if not isinstance(i, int):
            rcopy(slot, slot, zs.at[0], zr.at[d], other).wait_recv()
        rcopy(slot, slot, xs.at[0], xr.at[1, i], dev(z, pair, y, core)).start()
        rcopy(slot, slot, xs.at[0], xr.at[2, i], dev(z, cross, y, core)).start()
        spread(0, i, zsrc, mine)

    def from_x(i, o):
        zsrc = source(i)
        idx = piece(origin[o], par, core)
        slot = lat.at[zsrc, idx]
        rcopy(slot, slot, xs.at[0], xr.at[o, i], other).wait_recv()
        if o == 1:
            rcopy(slot, slot, xs.at[0], xr.at[3, i], dev(z, cross, y, core)).start()
        spread(o, i, zsrc, idx)

    def from_y(i):
        zsrc = source(i)
        for o in range(4):
            idx = piece(origin[o], 1 - par, core)
            slot = lat.at[zsrc, idx]
            rcopy(slot, slot, ys.at[0], yr.at[o, i], other).wait_recv()
            rcopy(slot, slot, ks.at[0], kr.at[0], other).start()

    def stage(m, carry):
        @pl.when(m < 4)
        def _():
            from_z(2 * m + 1)

        @pl.when(m < 3)
        def _():
            from_z(2 * m + 2)

        @pl.when(m < 8)
        def _():
            from_x(m, 1)
            from_x(m, 2)

        @pl.when(jnp.logical_and(m >= 1, m < 9))
        def _():
            from_x(m - 1, 3)

        @pl.when(m >= 3)
        def _():
            from_y(m - 3)

        return carry

    pl.semaphore_wait(barrier, 38)

    for d in (1, 7, 2, 6, 3, 5, 4):
        rcopy(lat.at[z, mine], lat.at[z, mine], zs.at[0], zr.at[d], zdev(d)).start()

    from_z(0)

    wj = lax.rem(z, 4)
    keeper = z // 4
    at_home = jnp.logical_and(core == xl, core == keeper)

    @pl.when(at_home)
    def _():
        pltpu.make_async_copy(w_hbm, wbuf.at[wj, xl], wr.at[wj, xl]).start()

    @pl.when(jnp.logical_not(at_home))
    def _():
        rcopy(
            w_hbm, wbuf.at[wj, xl], w0.at[0], wr.at[wj, xl], dev(z, xh * 2 + core, y, keeper)
        ).start()

    def place_of(b, carry):
        found = jnp.int32(0)
        for c in range(32):
            found = jnp.where(jnp.minimum(plan_ref[0, c], plan_ref[1, c]) == b, c, found)
        place[b] = found
        return carry

    loads[4].wait()
    lax.fori_loop(0, 32, place_of, 0)

    for cp in loads[1:4]:
        cp.wait()
    for h in range(HEAD_LOCAL):
        lo = h * (NOPE + ROPE)
        qn = qv[:, lo : lo + NOPE]
        qr = qv[:, lo + NOPE : lo + NOPE + ROPE].astype(jnp.float32) * SCALE2
        qr = qr.astype(jnp.bfloat16)
        ql = (nt(qn, kuv[:, h * NOPE : (h + 1) * NOPE]) * SCALE2).astype(jnp.bfloat16)
        qr = jnp.concatenate([qr, qr], axis=1)
        for i in range(2):
            qs[i, h * BLOCK : (h + 1) * BLOCK, 0:LATENT] = ql[i * BLOCK : (i + 1) * BLOCK]
            qs[i, h * BLOCK : (h + 1) * BLOCK, LATENT:WIDE] = qr[i * BLOCK : (i + 1) * BLOCK]

    def ring_send(j, part, up):
        slot = wbuf.at[j, part]
        n = 0 if up else 1
        rcopy(slot, slot, ws.at[n, j, part], wr.at[j, part], zdev(1 if up else 7)).start()

    def ring_wait(j, part):
        slot = wbuf.at[j, part]
        rcopy(slot, slot, w0.at[0], wr.at[j, part], other).wait_recv()

    def ring_moves(s, q):
        part = xl if q == 0 else 1 - xl
        for up in (True, False):
            reach = jnp.where((part == 0) == up, 4, 3)
            yield up, part, lax.rem(z + (8 - s if up else s), 8), reach

    def ring_step(s, q):
        if s == 0:
            part = xl if q == 0 else 1 - xl

            @pl.when(core == keeper)
            def _():
                ring_wait(wj, part)
                ring_send(wj, part, True)
                ring_send(wj, part, False)
            return
        for up, part, zsrc, reach in ring_moves(s, q):
            j = lax.rem(zsrc, 4)

            @pl.when(jnp.logical_and(core == zsrc // 4, s <= reach))
            def _():
                ring_wait(j, part)

            @pl.when(jnp.logical_and(core == zsrc // 4, s < reach))
            def _():
                ring_send(j, part, up)

    ring_step(0, 0)
    lax.fori_loop(0, 2, stage, 0)
    ring_step(0, 1)
    lax.fori_loop(2, 3, stage, 0)
    ring_step(1, 0)
    lax.fori_loop(3, 6, stage, 0)
    ring_step(1, 1)
    lax.fori_loop(6, 9, stage, 0)
    ring_step(2, 0)
    lax.fori_loop(9, 11, stage, 0)

    many = lat.at[pl.ds(0, 4)]
    rcopy(many, many, ks.at[0], kr.at[0], other).wait_recv()
    ring_step(2, 1)

    p0 = plan_ref[0, ctx]
    p1 = plan_ref[1, ctx]
    low = jnp.minimum(p0, p1)
    high = jnp.maximum(p0, p1)
    low_at = jnp.where(p0 < p1, 0, 1)
    beta = lax.div(low, 4)
    ahead = lax.broadcasted_iota(jnp.int32, (BLOCK, 256), 1) - lax.broadcasted_iota(
        jnp.int32, (BLOCK, 256), 0
    )
    left = lax.broadcasted_iota(jnp.int32, (16, 128), 1) < 64
    none = jnp.zeros((16, 128), jnp.bfloat16)

    def chunk_of(t):
        return jnp.where(t <= beta, t, t - beta - 1)

    def pieces_of(t):
        first = chunk_of(t) * 4
        got = []
        for i in range(4):
            c = place[jnp.minimum(first + i, 63 - first - i)]
            s = 2 * c + jnp.where(plan_ref[0, c] == first + i, 0, 1)
            pair = lat[lax.div(s, 8), pl.ds(lax.rem(s, 8) * 2, 2)]
            got += [pair[0], pair[1]]
        return got

    def wide_of(got):
        return jnp.concatenate(
            [
                jnp.concatenate([p[c * 32 : (c + 1) * 32] for p in got], axis=0)
                for c in range(4)
            ],
            axis=1,
        )

    def keys_of(t):
        got = pieces_of(t)
        rope = []
        for p in got:
            r = p[128:PIECE]
            rope += [jnp.where(left, r, none), jnp.where(left, none, r)]
        return jnp.concatenate([wide_of(got), jnp.concatenate(rope, axis=0)], axis=1)

    def values_of(t):
        return wide_of(pieces_of(t))

    def masked(s, first_row, first_key):
        allowed = (ahead <= first_row - first_key)[None]
        return jnp.where(allowed, s.reshape(HEAD_LOCAL, BLOCK, 256), NEG).reshape(ROWS, 256)

    def fold(s):
        return jnp.maximum(s[:, :128], s[:, 128:])

    mrun[0] = jnp.full((ROWS, 128), NEG, jnp.float32)
    lrun[0] = jnp.zeros((ROWS, 128), jnp.float32)
    acc[0] = jnp.zeros((ROWS, LATENT), jnp.float32)

    def score(t, carry):
        is_low = t <= beta
        q = qs[jnp.where(is_low, low_at, 1 - low_at)]
        s = nt(q, keys_of(t))
        s = masked(s, jnp.where(is_low, low, high) * BLOCK, chunk_of(t) * 256)
        sbuf[t] = s
        before = jnp.where(t == beta + 1, NEG, mrun[t])
        mrun[t + 1] = jnp.maximum(before, fold(s))
        return carry

    def row_max(at):
        return jnp.broadcast_to(jnp.max(mrun[at], axis=1, keepdims=True), (ROWS, 128))

    def weights(s, m):
        wa = jnp.exp2(s[:, :128] - m)
        wb = jnp.exp2(s[:, 128:] - m)
        return wa + wb, jnp.concatenate([wa, wb], axis=1).astype(jnp.bfloat16)

    def weigh(t, carry):
        is_low = t <= beta
        keep = jnp.where(t == beta + 1, 0.0, 1.0)
        total, w = weights(sbuf[t], mfin[jnp.where(is_low, 0, 1)])
        lrun[t + 1] = lrun[t] * keep + total
        added = jnp.dot(w, values_of(t), preferred_element_type=jnp.float32)
        acc[t + 1] = acc[t] * keep + added
        return carry

    def normal(at):
        total = jnp.sum(lrun[at], axis=1, keepdims=True)
        return (acc[at] / total).astype(jnp.bfloat16)

    def shard(half, src_x, c_):
        return att.at[half, lax.rem(src_x, 2) * 4 + (src_x // 2) * 2 + c_]

    def finish(half, o):
        for h in range(HEAD_LOCAL):
            up = jnp.dot(
                o[h * BLOCK : (h + 1) * BLOCK],
                vuv[:, h * VDIM : (h + 1) * VDIM],
                preferred_element_type=jnp.float32,
            )
            att[half, xl * 4 + xh * 2 + core, :, h * VDIM : (h + 1) * VDIM] = up.astype(jnp.bfloat16)
        here = shard(half, x, core)
        for n in (2, 1, 3):
            rcopy(here, here, as_.at[half], ar.at[half, n], xdev(n)).start()
        rcopy(here, here, bs.at[half], br.at[half], other).start()

    def pass_on(half):
        for n in (1, 3, 2):
            there = shard(half, lax.rem(x + 4 - n, 4), core)
            rcopy(there, there, as_.at[half], ar.at[half, n], other).wait_recv()
            rcopy(there, there, bs.at[half], br.at[half], other).start()

    def gathered(half):
        four = att.at[half, pl.ds(0, 4)]
        rcopy(four, four, bs.at[half], br.at[half], other).wait_recv()

    lax.fori_loop(0, EARLY, score, 0, unroll=3)
    mfin[0] = row_max(beta + 1)
    mfin[1] = row_max(EARLY)
    lax.fori_loop(0, EARLY, weigh, 0, unroll=3)
    finish(0, normal(beta + 1))
    ring_step(3, 0)

    def late_score(i, carry, last=False):
        t = EARLY + i
        s = nt(qs[1 - low_at], keys_of(t))
        if last:
            s = masked(s, high * BLOCK, chunk_of(t) * 256)
        sbuf[i] = s
        mrun[t + 1] = jnp.maximum(mrun[t], fold(s))
        return carry

    lax.fori_loop(0, LATE - 2, late_score, 0, unroll=3)
    late_score(LATE - 2, 0)
    late_score(LATE - 1, 0, last=True)
    mfin[0] = row_max(EARLY + LATE)
    again = jnp.exp2(mfin[1] - mfin[0])
    lrun[EARLY] = lrun[EARLY] * again
    acc[EARLY] = acc[EARLY] * jnp.concatenate([again] * 4, axis=1)

    def late_weigh(i, carry):
        m = mfin[0]
        total, w = weights(sbuf[2 * i], m)
        total2, w2 = weights(sbuf[2 * i + 1], m)
        lrun[EARLY] = lrun[EARLY] + (total + total2)
        v = jnp.concatenate([values_of(EARLY + 2 * i), values_of(EARLY + 2 * i + 1)], axis=0)
        acc[EARLY] = acc[EARLY] + jnp.dot(
            jnp.concatenate([w, w2], axis=1), v, preferred_element_type=jnp.float32
        )
        return carry

    lax.fori_loop(0, LATE // 2, late_weigh, 0, unroll=2)
    ring_step(3, 1)
    finish(1, normal(EARLY))
    pass_on(0)

    def pack(half, j, total):
        total = total.astype(jnp.bfloat16)
        for n in range(4):
            lanes = total[:, n * BLOCK : (n + 1) * BLOCK]
            csend[half, j * 4 + n] = jnp.concatenate([lanes[:112], lanes[112:]], axis=1)

    def rows_of(half, part):
        return att[half, part * 4 : part * 4 + 4].reshape(256, 1024)

    def project(j):
        pack(0, j, nt(wbuf[j, 0], rows_of(0, 0)) + nt(wbuf[j, 1], rows_of(0, 1)))

        @pl.when(j != y)
        def _():
            rcopy(
                csend.at[0, pl.ds(4 * j, 4)], crecv.at[0, pl.ds(4 * lax.rem(j + 4 - y, 4), 4)],
                cs.at[0], cr.at[0], dev(z, x, j, core),
            ).start()

    def by_distance(i):
        return lax.rem(y + 2 + jnp.where(i == 0, 0, jnp.where(i == 3, 2, 2 * i - 3)), 4)

    across = lax.rem(z + 4, 8)

    def early_columns(i, carry):
        j = by_distance(i)

        @pl.when(4 * core + j != across)
        def _():
            project(j)

        return carry

    gathered(0)
    lax.fori_loop(0, 4, early_columns, 0)
    ring_step(4, 0)
    ring_step(4, 1)

    @pl.when(core == across // 4)
    def _():
        project(lax.rem(across, 4))

    pass_on(1)
    gathered(1)

    def deliver(i, carry):
        j = by_distance(i)
        for n in range(4):
            at = lax.rem(n + 2 - 2 * xh, 4)
            to_x = (at // 2) * 2 + core
            to_core = lax.rem(at, 2)
            local = jnp.logical_and(jnp.logical_and(to_x == x, core == to_core), j == y)

            @pl.when(local)
            def _():
                pltpu.make_async_copy(
                    csend.at[1, j * 4 + at], crecv.at[1, y * 4 + x], cr.at[1]
                ).start()

            @pl.when(jnp.logical_not(local))
            def _():
                rcopy(
                    csend.at[1, j * 4 + at], crecv.at[1, y * 4 + x], cs.at[1],
                    cr.at[1], dev(z, to_x, j, to_core),
                ).start()
        return carry

    total = nt(wbuf[:, 0].reshape(896, 1024), rows_of(1, 0)) + nt(
        wbuf[:, 1].reshape(896, 1024), rows_of(1, 1)
    )
    for j in range(4):
        pack(1, j, total[j * 224 : (j + 1) * 224])
    lax.fori_loop(0, 4, deliver, 0)

    for part, sem in (
        (lat.at[pl.ds(0, 7), 0], zs.at[0]),
        (lat.at[pl.ds(0, 3), pl.ds(0, 8)], xs.at[0]),
        (lat.at[pl.ds(0, 2)], ys.at[0]),
        (lat.at[pl.ds(0, 4)], ks.at[0]),
    ):
        rcopy(part, part, sem, kr.at[0], other).wait_send()

    @pl.when(jnp.logical_not(at_home))
    def _():
        rcopy(w_hbm, wbuf.at[wj, xl], w0.at[0], wr.at[wj, xl], other).wait_send()

    for q in range(2):
        part = xl if q == 0 else 1 - xl

        @pl.when(core == keeper)
        def _():
            for n in range(2):
                slot = wbuf.at[wj, part]
                rcopy(slot, slot, ws.at[n, wj, part], wr.at[wj, part], other).wait_send()

        for s in range(1, 4):
            for up, part, zsrc, reach in ring_moves(s, q):
                j = lax.rem(zsrc, 4)

                @pl.when(jnp.logical_and(core == zsrc // 4, s < reach))
                def _():
                    slot = wbuf.at[j, part]
                    rcopy(
                        slot, slot, ws.at[0 if up else 1, j, part], wr.at[j, part], other
                    ).wait_send()

    three = crecv.at[0, pl.ds(4, 12)]
    rcopy(three, three, cs.at[0], cr.at[0], other).wait_recv()
    total = csend[0, pl.ds(4 * y, 4)].astype(jnp.float32)
    for o in range(1, 4):
        total = total + crecv[0, 4 * o : 4 * o + 4].astype(jnp.float32)
    fsend[...] = total.astype(jnp.bfloat16)
    for n in range(4):
        to_x = (n // 2) * 2 + core
        local = jnp.logical_and(to_x == x, core == n % 2)

        @pl.when(local)
        def _():
            pltpu.make_async_copy(fsend.at[n], frecv.at[x], fr.at[0]).start()

        @pl.when(jnp.logical_not(local))
        def _():
            rcopy(
                fsend.at[n], frecv.at[x], fs.at[0], fr.at[0], dev(z, to_x, y, n % 2)
            ).start()

    def columns_of(parts):
        sides = []
        for part in parts:
            sides += [part[:, :BLOCK], part[:, BLOCK:]]
        return jnp.concatenate(sides, axis=0)

    rcopy(frecv, frecv, fs.at[0], fr.at[0], other).wait_recv()
    low_rows = columns_of([frecv[n] for n in range(4)])
    rcopy(crecv.at[1], crecv.at[1], cs.at[1], cr.at[1], other).wait_recv()
    sums = []
    for n in range(4):
        total = crecv[1, n].astype(jnp.float32)
        for m in range(1, 4):
            total = total + crecv[1, m * 4 + n].astype(jnp.float32)
        sums.append(total.astype(jnp.bfloat16))
    high_rows = columns_of(sums)
    first = jnp.where(low_at == 0, low_rows, high_rows)
    second = jnp.where(low_at == 0, high_rows, low_rows)
    out_ref[...] = jnp.transpose(jnp.concatenate([first, second], axis=1), (1, 0))

    for half in range(2):
        for count, sem in ((3, as_.at[half]), (4, bs.at[half])):
            some = att.at[half, pl.ds(0, count)]
            rcopy(some, some, sem, br.at[half], other).wait_send()
    rcopy(three, three, cs.at[0], cr.at[0], other).wait_send()

    @pl.when(core == xl)
    def _():
        home = fsend.at[pl.ds(0, 3)]
        rcopy(home, home, fs.at[0], fr.at[0], other).wait_send()
        sent = csend.at[1, pl.ds(0, 15)]
        rcopy(sent, sent, cs.at[1], cr.at[1], other).wait_send()

    @pl.when(core != xl)
    def _():
        rcopy(fsend, fsend, fs.at[0], fr.at[0], other).wait_send()
        rcopy(csend.at[1], csend.at[1], cs.at[1], cr.at[1], other).wait_send()


def body(queries, latent_rope, key_up, value_up, out_weight, plan):
    vm = pl.BlockSpec(memory_space=pltpu.VMEM)
    anywhere = pl.BlockSpec(memory_space=pl.ANY)
    bf, f32 = jnp.bfloat16, jnp.float32
    dma = pltpu.SemaphoreType.DMA
    return pl.pallas_call(
        kernel,
        out_shape=jax.ShapeDtypeStruct((128, 896), bf),
        in_specs=[anywhere, anywhere, anywhere, anywhere, anywhere, anywhere],
        out_specs=vm,
        scratch_shapes=[
            pltpu.SMEM((2, 32), jnp.int32),
            pltpu.SMEM((32,), jnp.int32),
            pltpu.VMEM((LATENT + ROPE, 128), bf),
            pltpu.VMEM((8, 16, PIECE, 128), bf),
            pltpu.VMEM((128, 1536), bf),
            pltpu.VMEM((512, 1024), bf),
            pltpu.VMEM((512, 1024), bf),
            pltpu.VMEM((2, ROWS, WIDE), bf),
            pltpu.VMEM((EARLY, ROWS, 256), f32),
            pltpu.VMEM((EARLY + LATE + 1, ROWS, 128), f32),
            pltpu.VMEM((2, ROWS, 128), f32),
            pltpu.VMEM((EARLY + 1, ROWS, 128), f32),
            pltpu.VMEM((EARLY + 1, ROWS, LATENT), f32),
            pltpu.VMEM((4, 2, 224, 1024), bf),
            pltpu.VMEM((2, 8, BLOCK, 1024), bf),
            pltpu.VMEM((2, 16, 112, 128), bf),
            pltpu.VMEM((2, 16, 112, 128), bf),
            pltpu.VMEM((4, 112, 128), bf),
            pltpu.VMEM((4, 112, 128), bf),
            dma((5,)), dma((1,)), dma((8,)), dma((1,)), dma((4, 8)), dma((1,)), dma((4, 8)),
            dma((1,)), dma((1,)), dma((1,)), dma((2, 4, 2)), dma((4, 2)),
            dma((2,)), dma((2, 4)), dma((2,)), dma((2,)), dma((2,)), dma((2,)), dma((1,)), dma((1,)),
        ],
        compiler_params=pltpu.CompilerParams(
            collective_id=0, has_side_effects=True, vmem_limit_bytes=56 * 2**20
        ),
    )(plan.T, latent_rope.T, queries, key_up, value_up, out_weight.T)


def solution(mesh):
    placed = (
        P("ctx", "head"),
        P("ctx", None),
        P(None, "head"),
        P(None, "head"),
        P("head", "ctx"),
        P(),
    )
    return jax.shard_map(
        body, mesh=mesh, in_specs=placed, out_specs=P("ctx", "head"), check_vma=False
    )
```

```python
import jax
import jax.numpy as jnp
from jax import lax
from jax.experimental import pallas as pl
from jax.experimental.pallas import tpu as pltpu
from jax.sharding import PartitionSpec as P

MESH = pl.DeviceIdType.MESH
NOPE = 128
ROPE = 64
VDIM = 128
LATENT = 512
HEAD_LOCAL = 8
BLOCK = 64
ROWS = HEAD_LOCAL * BLOCK
EARLY = 9
LATE = 8
WIDE = 640
PIECE = 144
NEG = -1e30
SCALE2 = 1.4426950408889634 * (NOPE + ROPE) ** -0.5


def nt(a, b):
    return lax.dot_general(a, b, (((1,), (1,)), ((), ())), preferred_element_type=jnp.float32)


def kernel(
    plan_hbm, lrt_hbm, q_hbm, ku_hbm, vu_hbm, w_hbm, out_ref,
    plan_ref, place, lrt, lat, qv, kuv, vuv, qs, sbuf, mrun, mfin, lrun, acc, wbuf, att, csend, crecv, fsend, frecv,
    ls, zs, zr, xs, xr, ys, yr, ks, kr, w0, ws, wr, as_, ar, bs, br, cs, cr, fs, fr,
):
    ctx = lax.axis_index("ctx")
    head = lax.axis_index("head")
    core = lax.rem(ctx, 2)
    xh = lax.rem(ctx // 2, 2)
    z = ctx // 4
    xl = head // 4
    y = lax.rem(head, 4)
    x = xh * 2 + xl

    def dev(z_, x_, y_, c_):
        return ((z_ * 2 + x_ // 2) * 2 + c_, lax.rem(x_, 2) * 4 + y_)

    def zdev(d):
        return dev(lax.rem(z + d, 8), x, y, core)

    def xdev(o):
        return dev(z, lax.rem(x + o, 4), y, core)

    def ydev(o):
        return dev(z, x, lax.rem(y + o, 4), core)

    other = dev(z, x, y, 1 - core)

    def rcopy(src, dst, ssem, rsem, target):
        return pltpu.make_async_remote_copy(
            src_ref=src, dst_ref=dst, send_sem=ssem, recv_sem=rsem,
            device_id=target, device_id_type=MESH,
        )

    loads = [
        pltpu.make_async_copy(lrt_hbm, lrt, ls.at[3]),
        pltpu.make_async_copy(q_hbm, qv, ls.at[0]),
        pltpu.make_async_copy(ku_hbm, kuv, ls.at[1]),
        pltpu.make_async_copy(vu_hbm, vuv, ls.at[2]),
        pltpu.make_async_copy(plan_hbm, plan_ref, ls.at[4]),
    ]
    for cp in loads:
        cp.start()

    barrier = pltpu.get_barrier_semaphore()
    for d in range(1, 8):
        pl.semaphore_signal(barrier, 1, device_id=zdev(d), device_id_type=MESH)
    for oy in range(4):
        for ox in range(4):
            for oc in range(2):
                if oy or ox or oc:
                    pl.semaphore_signal(
                        barrier, 1,
                        device_id=dev(z, lax.rem(x + ox, 4), lax.rem(y + oy, 4), lax.rem(core + oc, 2)),
                        device_id_type=MESH,
                    )
    par = lax.rem(y, 2)

    def piece(src_x, parity, c_):
        return (src_x // 2) * 8 + c_ * 4 + parity * 2 + lax.rem(src_x, 2)

    mine = piece(x, par, core)
    loads[0].wait()
    rows_all = jnp.transpose(lrt[...], (1, 0))
    quarter = par * 2 + xl
    for q in range(4):
        @pl.when(quarter == q)
        def _():
            part = rows_all[q * 32 : (q + 1) * 32]
            for c in range(4):
                lat[z, mine, c * 32 : (c + 1) * 32] = part[:, c * 128 : (c + 1) * 128]
            rope = part[:, LATENT:]
            lat[z, mine, 128:PIECE] = jnp.concatenate([rope[:16], rope[16:]], axis=1)

    def dist(i):
        if isinstance(i, int):
            return 0
        return lax.rem(jnp.where(lax.rem(i, 2) == 1, (i + 1) // 2, 8 - i // 2), 8)

    def source(i):
        return lax.rem(z + 8 - dist(i), 8)

    def spread(o, i, zsrc, idx):
        slot = lat.at[zsrc, idx]
        to = lax.rem(y + 1 + 2 * (i % 2), 4)
        rcopy(slot, slot, ys.at[0], yr.at[o, i], dev(z, x, to, core)).start()
        rcopy(slot, slot, ks.at[0], kr.at[0], other).start()

    pair = x + 1 - 2 * xl
    cross = 3 - x
    origin = (x, pair, cross, lax.rem(x + 2, 4))

    def from_z(i):
        zsrc = source(i)
        slot = lat.at[zsrc, mine]
        d = dist(i)

        if not isinstance(i, int):
            rcopy(slot, slot, zs.at[0], zr.at[d], other).wait_recv()
        rcopy(slot, slot, xs.at[0], xr.at[1, i], dev(z, pair, y, core)).start()
        rcopy(slot, slot, xs.at[0], xr.at[2, i], dev(z, cross, y, core)).start()
        spread(0, i, zsrc, mine)

    def from_x(i, o):
        zsrc = source(i)
        idx = piece(origin[o], par, core)
        slot = lat.at[zsrc, idx]
        rcopy(slot, slot, xs.at[0], xr.at[o, i], other).wait_recv()
        if o == 1:
            rcopy(slot, slot, xs.at[0], xr.at[3, i], dev(z, cross, y, core)).start()
        spread(o, i, zsrc, idx)

    def from_y(i):
        zsrc = source(i)
        for o in range(4):
            idx = piece(origin[o], 1 - par, core)
            slot = lat.at[zsrc, idx]
            rcopy(slot, slot, ys.at[0], yr.at[o, i], other).wait_recv()
            rcopy(slot, slot, ks.at[0], kr.at[0], other).start()

    def stage(m, carry):
        @pl.when(m < 4)
        def _():
            from_z(2 * m + 1)

        @pl.when(m < 3)
        def _():
            from_z(2 * m + 2)

        @pl.when(m < 8)
        def _():
            from_x(m, 1)
            from_x(m, 2)

        @pl.when(jnp.logical_and(m >= 1, m < 9))
        def _():
            from_x(m - 1, 3)

        @pl.when(m >= 3)
        def _():
            from_y(m - 3)

        return carry

    pl.semaphore_wait(barrier, 38)

    for d in (1, 7, 2, 6, 3, 5, 4):
        rcopy(lat.at[z, mine], lat.at[z, mine], zs.at[0], zr.at[d], zdev(d)).start()

    from_z(0)

    wj = lax.rem(z, 4)
    keeper = z // 4
    at_home = jnp.logical_and(core == xl, core == keeper)

    @pl.when(at_home)
    def _():
        pltpu.make_async_copy(w_hbm, wbuf.at[wj, xl], wr.at[wj, xl]).start()

    @pl.when(jnp.logical_not(at_home))
    def _():
        rcopy(
            w_hbm, wbuf.at[wj, xl], w0.at[0], wr.at[wj, xl], dev(z, xh * 2 + core, y, keeper)
        ).start()

    def place_of(b, carry):
        found = jnp.int32(0)
        for c in range(32):
            found = jnp.where(lowers[c] == b, c, found)
        place[b] = found
        return carry

    loads[4].wait()
    lowers = [jnp.minimum(plan_ref[0, c], plan_ref[1, c]) for c in range(32)]
    lax.fori_loop(0, 32, place_of, 0)

    for cp in loads[1:4]:
        cp.wait()
    for h in range(HEAD_LOCAL):
        lo = h * (NOPE + ROPE)
        qn = qv[:, lo : lo + NOPE]
        qr = qv[:, lo + NOPE : lo + NOPE + ROPE].astype(jnp.float32) * SCALE2
        qr = qr.astype(jnp.bfloat16)
        ql = (nt(qn, kuv[:, h * NOPE : (h + 1) * NOPE]) * SCALE2).astype(jnp.bfloat16)
        qr = jnp.concatenate([qr, qr], axis=1)
        for i in range(2):
            qs[i, h * BLOCK : (h + 1) * BLOCK, 0:LATENT] = ql[i * BLOCK : (i + 1) * BLOCK]
            qs[i, h * BLOCK : (h + 1) * BLOCK, LATENT:WIDE] = qr[i * BLOCK : (i + 1) * BLOCK]

    def ring_send(j, part, up):
        slot = wbuf.at[j, part]
        n = 0 if up else 1
        rcopy(slot, slot, ws.at[n, j, part], wr.at[j, part], zdev(1 if up else 7)).start()

    def ring_wait(j, part):
        slot = wbuf.at[j, part]
        rcopy(slot, slot, w0.at[0], wr.at[j, part], other).wait_recv()

    def ring_moves(s, q):
        part = xl if q == 0 else 1 - xl
        for up in (True, False):
            reach = jnp.where((part == 0) == up, 4, 3)
            yield up, part, lax.rem(z + (8 - s if up else s), 8), reach

    def ring_step(s, q):
        if s == 0:
            part = xl if q == 0 else 1 - xl

            @pl.when(core == keeper)
            def _():
                ring_wait(wj, part)
                ring_send(wj, part, True)
                ring_send(wj, part, False)
            return
        for up, part, zsrc, reach in ring_moves(s, q):
            j = lax.rem(zsrc, 4)

            @pl.when(jnp.logical_and(core == zsrc // 4, s <= reach))
            def _():
                ring_wait(j, part)

            @pl.when(jnp.logical_and(core == zsrc // 4, s < reach))
            def _():
                ring_send(j, part, up)

    ring_step(0, 0)
    lax.fori_loop(0, 2, stage, 0)
    ring_step(0, 1)
    lax.fori_loop(2, 3, stage, 0)
    ring_step(1, 0)
    lax.fori_loop(3, 6, stage, 0)
    ring_step(1, 1)
    lax.fori_loop(6, 9, stage, 0)
    ring_step(2, 0)
    lax.fori_loop(9, 11, stage, 0)

    many = lat.at[pl.ds(0, 4)]
    rcopy(many, many, ks.at[0], kr.at[0], other).wait_recv()
    ring_step(2, 1)

    p0 = plan_ref[0, ctx]
    p1 = plan_ref[1, ctx]
    low = jnp.minimum(p0, p1)
    high = jnp.maximum(p0, p1)
    low_at = jnp.where(p0 < p1, 0, 1)
    beta = lax.div(low, 4)
    ahead = lax.broadcasted_iota(jnp.int32, (BLOCK, 256), 1) - lax.broadcasted_iota(
        jnp.int32, (BLOCK, 256), 0
    )
    left = lax.broadcasted_iota(jnp.int32, (16, 128), 1) < 64
    none = jnp.zeros((16, 128), jnp.bfloat16)

    def chunk_of(t):
        return jnp.where(t <= beta, t, t - beta - 1)

    def pieces_of(t):
        first = chunk_of(t) * 4
        got = []
        for i in range(4):
            c = place[jnp.minimum(first + i, 63 - first - i)]
            s = 2 * c + jnp.where(plan_ref[0, c] == first + i, 0, 1)
            pair = lat[lax.div(s, 8), pl.ds(lax.rem(s, 8) * 2, 2)]
            got += [pair[0], pair[1]]
        return got

    def wide_of(got):
        return jnp.concatenate(
            [
                jnp.concatenate([p[c * 32 : (c + 1) * 32] for p in got], axis=0)
                for c in range(4)
            ],
            axis=1,
        )

    def keys_of(t):
        got = pieces_of(t)
        rope = []
        for p in got:
            r = p[128:PIECE]
            rope += [jnp.where(left, r, none), jnp.where(left, none, r)]
        return jnp.concatenate([wide_of(got), jnp.concatenate(rope, axis=0)], axis=1)

    def values_of(t):
        return wide_of(pieces_of(t))

    def masked(s, first_row, first_key):
        allowed = (ahead <= first_row - first_key)[None]
        return jnp.where(allowed, s.reshape(HEAD_LOCAL, BLOCK, 256), NEG).reshape(ROWS, 256)

    def fold(s):
        return jnp.maximum(s[:, :128], s[:, 128:])

    mrun[0] = jnp.full((ROWS, 128), NEG, jnp.float32)
    lrun[0] = jnp.zeros((ROWS, 128), jnp.float32)
    acc[0] = jnp.zeros((ROWS, LATENT), jnp.float32)

    def score(t, carry):
        is_low = t <= beta
        q = qs[jnp.where(is_low, low_at, 1 - low_at)]
        s = nt(q, keys_of(t))
        s = masked(s, jnp.where(is_low, low, high) * BLOCK, chunk_of(t) * 256)
        sbuf[t] = s
        before = jnp.where(t == beta + 1, NEG, mrun[t])
        mrun[t + 1] = jnp.maximum(before, fold(s))
        return carry

    def row_max(at):
        return jnp.broadcast_to(jnp.max(mrun[at], axis=1, keepdims=True), (ROWS, 128))

    def weights(s, m):
        wa = jnp.exp2(s[:, :128] - m)
        wb = jnp.exp2(s[:, 128:] - m)
        return wa + wb, jnp.concatenate([wa, wb], axis=1).astype(jnp.bfloat16)

    def weigh(t, carry):
        is_low = t <= beta
        keep = jnp.where(t == beta + 1, 0.0, 1.0)
        total, w = weights(sbuf[t], mfin[jnp.where(is_low, 0, 1)])
        lrun[t + 1] = lrun[t] * keep + total
        added = jnp.dot(w, values_of(t), preferred_element_type=jnp.float32)
        acc[t + 1] = acc[t] * keep + added
        return carry

    def normal(at):
        total = jnp.sum(lrun[at], axis=1, keepdims=True)
        return (acc[at] / total).astype(jnp.bfloat16)

    def shard(half, src_x, c_):
        return att.at[half, lax.rem(src_x, 2) * 4 + (src_x // 2) * 2 + c_]

    def finish(half, o):
        for h in range(HEAD_LOCAL):
            up = jnp.dot(
                o[h * BLOCK : (h + 1) * BLOCK],
                vuv[:, h * VDIM : (h + 1) * VDIM],
                preferred_element_type=jnp.float32,
            )
            att[half, xl * 4 + xh * 2 + core, :, h * VDIM : (h + 1) * VDIM] = up.astype(jnp.bfloat16)
        here = shard(half, x, core)
        for n in (2, 1, 3):
            rcopy(here, here, as_.at[half], ar.at[half, n], xdev(n)).start()
        rcopy(here, here, bs.at[half], br.at[half], other).start()

    def pass_on(half):
        for n in (1, 3, 2):
            there = shard(half, lax.rem(x + 4 - n, 4), core)
            rcopy(there, there, as_.at[half], ar.at[half, n], other).wait_recv()
            rcopy(there, there, bs.at[half], br.at[half], other).start()

    def gathered(half):
        four = att.at[half, pl.ds(0, 4)]
        rcopy(four, four, bs.at[half], br.at[half], other).wait_recv()

    lax.fori_loop(0, EARLY, score, 0, unroll=3)
    mfin[0] = row_max(beta + 1)
    mfin[1] = row_max(EARLY)
    lax.fori_loop(0, EARLY, weigh, 0, unroll=3)
    finish(0, normal(beta + 1))
    ring_step(3, 0)

    def late_score(i, carry, last=False):
        t = EARLY + i
        s = nt(qs[1 - low_at], keys_of(t))
        if last:
            s = masked(s, high * BLOCK, chunk_of(t) * 256)
        sbuf[i] = s
        mrun[t + 1] = jnp.maximum(mrun[t], fold(s))
        return carry

    lax.fori_loop(0, LATE - 2, late_score, 0, unroll=3)
    late_score(LATE - 2, 0)
    late_score(LATE - 1, 0, last=True)
    mfin[0] = row_max(EARLY + LATE)
    again = jnp.exp2(mfin[1] - mfin[0])
    lrun[EARLY] = lrun[EARLY] * again
    acc[EARLY] = acc[EARLY] * jnp.concatenate([again] * 4, axis=1)

    def late_weigh(i, carry):
        m = mfin[0]
        total, w = weights(sbuf[2 * i], m)
        total2, w2 = weights(sbuf[2 * i + 1], m)
        lrun[EARLY] = lrun[EARLY] + (total + total2)
        v = jnp.concatenate([values_of(EARLY + 2 * i), values_of(EARLY + 2 * i + 1)], axis=0)
        acc[EARLY] = acc[EARLY] + jnp.dot(
            jnp.concatenate([w, w2], axis=1), v, preferred_element_type=jnp.float32
        )
        return carry

    lax.fori_loop(0, LATE // 2, late_weigh, 0, unroll=2)
    ring_step(3, 1)
    finish(1, normal(EARLY))
    pass_on(0)

    def pack(half, j, total):
        total = total.astype(jnp.bfloat16)
        for n in range(4):
            lanes = total[:, n * BLOCK : (n + 1) * BLOCK]
            csend[half, j * 4 + n] = jnp.concatenate([lanes[:112], lanes[112:]], axis=1)

    def rows_of(half, part):
        return att[half, part * 4 : part * 4 + 4].reshape(256, 1024)

    def project(j):
        pack(0, j, nt(wbuf[j, 0], rows_of(0, 0)) + nt(wbuf[j, 1], rows_of(0, 1)))

        @pl.when(j != y)
        def _():
            rcopy(
                csend.at[0, pl.ds(4 * j, 4)], crecv.at[0, pl.ds(4 * lax.rem(j + 4 - y, 4), 4)],
                cs.at[0], cr.at[0], dev(z, x, j, core),
            ).start()

    def by_distance(i):
        return lax.rem(y + 2 + jnp.where(i == 0, 0, jnp.where(i == 3, 2, 2 * i - 3)), 4)

    across = lax.rem(z + 4, 8)

    def early_columns(i, carry):
        j = by_distance(i)

        @pl.when(4 * core + j != across)
        def _():
            project(j)

        return carry

    gathered(0)
    lax.fori_loop(0, 4, early_columns, 0)
    ring_step(4, 0)
    ring_step(4, 1)

    @pl.when(core == across // 4)
    def _():
        project(lax.rem(across, 4))

    pass_on(1)
    gathered(1)

    def deliver(i, carry):
        j = by_distance(i)
        for n in range(4):
            at = lax.rem(n + 2 - 2 * xh, 4)
            to_x = (at // 2) * 2 + core
            to_core = lax.rem(at, 2)
            local = jnp.logical_and(jnp.logical_and(to_x == x, core == to_core), j == y)

            @pl.when(local)
            def _():
                pltpu.make_async_copy(
                    csend.at[1, j * 4 + at], crecv.at[1, y * 4 + x], cr.at[1]
                ).start()

            @pl.when(jnp.logical_not(local))
            def _():
                rcopy(
                    csend.at[1, j * 4 + at], crecv.at[1, y * 4 + x], cs.at[1],
                    cr.at[1], dev(z, to_x, j, to_core),
                ).start()
        return carry

    total = nt(wbuf[:, 0].reshape(896, 1024), rows_of(1, 0)) + nt(
        wbuf[:, 1].reshape(896, 1024), rows_of(1, 1)
    )
    for j in range(4):
        pack(1, j, total[j * 224 : (j + 1) * 224])
    lax.fori_loop(0, 4, deliver, 0)

    for part, sem in (
        (lat.at[pl.ds(0, 7), 0], zs.at[0]),
        (lat.at[pl.ds(0, 3), pl.ds(0, 8)], xs.at[0]),
        (lat.at[pl.ds(0, 2)], ys.at[0]),
        (lat.at[pl.ds(0, 4)], ks.at[0]),
    ):
        rcopy(part, part, sem, kr.at[0], other).wait_send()

    @pl.when(jnp.logical_not(at_home))
    def _():
        rcopy(w_hbm, wbuf.at[wj, xl], w0.at[0], wr.at[wj, xl], other).wait_send()

    for q in range(2):
        part = xl if q == 0 else 1 - xl

        @pl.when(core == keeper)
        def _():
            for n in range(2):
                slot = wbuf.at[wj, part]
                rcopy(slot, slot, ws.at[n, wj, part], wr.at[wj, part], other).wait_send()

        for s in range(1, 4):
            for up, part, zsrc, reach in ring_moves(s, q):
                j = lax.rem(zsrc, 4)

                @pl.when(jnp.logical_and(core == zsrc // 4, s < reach))
                def _():
                    slot = wbuf.at[j, part]
                    rcopy(
                        slot, slot, ws.at[0 if up else 1, j, part], wr.at[j, part], other
                    ).wait_send()

    three = crecv.at[0, pl.ds(4, 12)]
    rcopy(three, three, cs.at[0], cr.at[0], other).wait_recv()
    total = csend[0, pl.ds(4 * y, 4)].astype(jnp.float32)
    for o in range(1, 4):
        total = total + crecv[0, 4 * o : 4 * o + 4].astype(jnp.float32)
    fsend[...] = total.astype(jnp.bfloat16)
    for n in range(4):
        to_x = (n // 2) * 2 + core
        local = jnp.logical_and(to_x == x, core == n % 2)

        @pl.when(local)
        def _():
            pltpu.make_async_copy(fsend.at[n], frecv.at[x], fr.at[0]).start()

        @pl.when(jnp.logical_not(local))
        def _():
            rcopy(
                fsend.at[n], frecv.at[x], fs.at[0], fr.at[0], dev(z, to_x, y, n % 2)
            ).start()

    def columns_of(parts):
        sides = []
        for part in parts:
            sides += [part[:, :BLOCK], part[:, BLOCK:]]
        return jnp.concatenate(sides, axis=0)

    rcopy(frecv, frecv, fs.at[0], fr.at[0], other).wait_recv()
    low_rows = columns_of([frecv[n] for n in range(4)])
    rcopy(crecv.at[1], crecv.at[1], cs.at[1], cr.at[1], other).wait_recv()
    sums = []
    for n in range(4):
        total = crecv[1, n].astype(jnp.float32)
        for m in range(1, 4):
            total = total + crecv[1, m * 4 + n].astype(jnp.float32)
        sums.append(total.astype(jnp.bfloat16))
    high_rows = columns_of(sums)
    first = jnp.where(low_at == 0, low_rows, high_rows)
    second = jnp.where(low_at == 0, high_rows, low_rows)
    out_ref[...] = jnp.transpose(jnp.concatenate([first, second], axis=1), (1, 0))

    for half in range(2):
        for count, sem in ((3, as_.at[half]), (4, bs.at[half])):
            some = att.at[half, pl.ds(0, count)]
            rcopy(some, some, sem, br.at[half], other).wait_send()
    rcopy(three, three, cs.at[0], cr.at[0], other).wait_send()

    @pl.when(core == xl)
    def _():
        home = fsend.at[pl.ds(0, 3)]
        rcopy(home, home, fs.at[0], fr.at[0], other).wait_send()
        sent = csend.at[1, pl.ds(0, 15)]
        rcopy(sent, sent, cs.at[1], cr.at[1], other).wait_send()

    @pl.when(core != xl)
    def _():
        rcopy(fsend, fsend, fs.at[0], fr.at[0], other).wait_send()
        rcopy(csend.at[1], csend.at[1], cs.at[1], cr.at[1], other).wait_send()


def body(queries, latent_rope, key_up, value_up, out_weight, plan):
    vm = pl.BlockSpec(memory_space=pltpu.VMEM)
    anywhere = pl.BlockSpec(memory_space=pl.ANY)
    bf, f32 = jnp.bfloat16, jnp.float32
    dma = pltpu.SemaphoreType.DMA
    return pl.pallas_call(
        kernel,
        out_shape=jax.ShapeDtypeStruct((128, 896), bf),
        in_specs=[anywhere, anywhere, anywhere, anywhere, anywhere, anywhere],
        out_specs=vm,
        scratch_shapes=[
            pltpu.SMEM((2, 32), jnp.int32),
            pltpu.SMEM((32,), jnp.int32),
            pltpu.VMEM((LATENT + ROPE, 128), bf),
            pltpu.VMEM((8, 16, PIECE, 128), bf),
            pltpu.VMEM((128, 1536), bf),
            pltpu.VMEM((512, 1024), bf),
            pltpu.VMEM((512, 1024), bf),
            pltpu.VMEM((2, ROWS, WIDE), bf),
            pltpu.VMEM((EARLY, ROWS, 256), f32),
            pltpu.VMEM((EARLY + LATE + 1, ROWS, 128), f32),
            pltpu.VMEM((2, ROWS, 128), f32),
            pltpu.VMEM((EARLY + 1, ROWS, 128), f32),
            pltpu.VMEM((EARLY + 1, ROWS, LATENT), f32),
            pltpu.VMEM((4, 2, 224, 1024), bf),
            pltpu.VMEM((2, 8, BLOCK, 1024), bf),
            pltpu.VMEM((2, 16, 112, 128), bf),
            pltpu.VMEM((2, 16, 112, 128), bf),
            pltpu.VMEM((4, 112, 128), bf),
            pltpu.VMEM((4, 112, 128), bf),
            dma((5,)), dma((1,)), dma((8,)), dma((1,)), dma((4, 8)), dma((1,)), dma((4, 8)),
            dma((1,)), dma((1,)), dma((1,)), dma((2, 4, 2)), dma((4, 2)),
            dma((2,)), dma((2, 4)), dma((2,)), dma((2,)), dma((2,)), dma((2,)), dma((1,)), dma((1,)),
        ],
        compiler_params=pltpu.CompilerParams(
            collective_id=0, has_side_effects=True, vmem_limit_bytes=56 * 2**20
        ),
    )(plan.T, latent_rope.T, queries, key_up, value_up, out_weight.T)


def solution(mesh):
    placed = (
        P("ctx", "head"),
        P("ctx", None),
        P(None, "head"),
        P(None, "head"),
        P("head", "ctx"),
        P(),
    )
    return jax.shard_map(
        body, mesh=mesh, in_specs=placed, out_specs=P("ctx", "head"), check_vma=False
    )
```
